128 devices in a mesh: chan: 8 (over z, y_hi), tblk: 16 (over y_lo, x, core).
Axes of the slice: x: 4, y: 4 (y_hi: 2, y_lo: 2; y = y_hi * 2 + y_lo), z: 4, core: 2. Of those that a mesh axis runs over, the one named last changes fastest.
Arguments:
- sky_image: float32 [8, 512, 1024], P(None, 'tblk', 'chan'), may hold values from 0 to 2
- dual_coefs: float32 [9, 8, 512, 1024], P(None, None, 'tblk', 'chan'), may hold values from -3 to 3
- phase_screen: float32 [8, 16, 512, 1024], P('chan', 'tblk'), may hold values from -3.140625 to 3.140625
- grid_rows: int32 [8, 16, 64], P('chan', 'tblk'), may hold values from 0 to 511
- grid_weight: float32 [8, 16, 1024, 256], P('chan', 'tblk'), may hold values from -0.1875 to 0.1875
- visibilities: float32 [8, 16, 2, 64, 256], P('chan', 'tblk'), may hold values from -6 to 6
- filters: float32 [9, 2, 3], replicated, may hold values from -1 to 1
- level_counts: int32 [9], replicated, may hold values from 1 to 3, as said below
- radius: float32 [9], replicated, may hold values from 0.5 to 4
Outputs:
- sky_update: float32 [8, 512, 1024], P(None, 'tblk', 'chan')
- dual_update: float32 [9, 8, 512, 1024], P(None, None, 'tblk', 'chan')
The draws below stay inside these ranges and needn't reach their ends.
Inputs may be any that keep to these rules, and one draw needn't show every extreme that they name: `level_counts`: at least one basis has 3 levels.
All inputs are finite; a program needn't handle non-finite values.
Results may differ from the reference program's by a relative error of at most 0.00011.
Values sent between devices are 32-bit elements; how exact they have to be, the bound alone decides.
No kernel may reach another device: no remote copies, remote signals or barrier semaphores. Data moves between devices by JAX's collectives and lax.ppermute only.
A program may use at most 128 MiB of HBM per device.

```python
import math
import jax
import jax.numpy as jnp
from jax import lax

NX = 512
NY = 1024
RVIS = 64
VIS = 256
NBASIS = 9
LEVELS = 3
ITERS = 2
HALO = 4
CH = 8
NBLK = 16


def draw_level_counts(key, part):
    first_key = jax.random.fold_in(key, 11)
    second_key = jax.random.fold_in(key, 23)
    drawn = jax.random.randint(first_key, (NBASIS,), 1, LEVELS + 1)
    chosen = jax.random.randint(second_key, (), 0, NBASIS)
    return jnp.where(jnp.arange(NBASIS) == chosen, LEVELS, drawn).astype(jnp.int32)


def place_ends(values, own_key, least, top_value):
    shape = values.shape
    place = [jax.random.randint(jax.random.fold_in(own_key, axis), (), 0, shape[axis]) for axis in range(len(shape))]
    values = values.at[tuple(place)].set(least)
    longest = shape.index(max(shape))
    place[longest] = (place[longest] + 1) % shape[longest]
    return values.at[tuple(place)].set(top_value)


def shard_levels(rng, extent, shards, smallest, top_value):
    def one(dim, shards_of):
        heights = jax.random.uniform(jax.random.fold_in(jax.random.fold_in(rng, 6), dim), (shards_of,), jnp.float32, smallest / len(shards), top_value / len(shards))
        return jnp.repeat(jnp.exp(heights), extent[dim] // shards_of).reshape((-1,) + (1,) * (len(extent) - dim - 1))

    factor_of = one(*shards[0])
    for cut in shards[1:]:
        factor_of = factor_of * one(*cut)
    return factor_of


def centred(own_key, shape, scale, reach, split=(), kind=jnp.bfloat16):
    values = scale * jax.random.normal(own_key, shape, jnp.float32)
    if split:
        values = values * shard_levels(own_key, shape, split, -0.22, 0.18)
    return jnp.clip(values, -reach, reach).astype(kind)


def setup_inputs(seed: int = 0) -> dict:
    streams_of = jax.random.split(jax.random.key(seed), 10)
    return {
        "sky_image": jnp.clip(2.0 * jax.random.uniform(streams_of[0], (CH, NX, NY), jnp.float32) ** shard_levels(streams_of[0], (CH, NX, NY), ((1, 16), (2, 8)), -0.2, 0.2), 0.0, 2.0),
        "dual_coefs": centred(streams_of[1], (NBASIS, CH, NX, NY), 0.5, 3.0, ((2, 16), (3, 8)), jnp.float32),
        "phase_screen": jnp.clip(jax.random.uniform(streams_of[2], (CH, NBLK, NX, NY), jnp.float32, -3.140625, 3.140625), -3.140625, 3.140625),
        "grid_rows": place_ends(jax.random.randint(streams_of[3], (CH, NBLK, RVIS), 0, NX), jax.random.fold_in(streams_of[3], 1), 0, NX - 1).astype(jnp.int32),
        "grid_weight": centred(streams_of[4], (CH, NBLK, NY, VIS), NY ** -0.5, 0.1875, ((0, 8), (1, 16)), jnp.float32),
        "visibilities": centred(streams_of[5], (CH, NBLK, 2, RVIS, VIS), 1.0, 6.0, ((0, 8), (1, 16)), jnp.float32),
        "filters": jnp.clip(jax.random.uniform(streams_of[6], (NBASIS, 2, 3), jnp.float32, -1.0, 1.0), -1.0, 1.0),
        "level_counts": draw_level_counts(jax.random.fold_in(streams_of[9], 71), 0),
        "radius": jnp.clip(jnp.exp(jax.random.uniform(streams_of[8], (NBASIS,), jnp.float32, math.log(0.5), math.log(4.0))), 0.5, 4.0),
    }


FULL_PRECISION = lax.Precision.HIGHEST
STEP_PRIMAL = 0.5
STEP_DUAL = 0.5

def filter_forward(padded, filter_taps, stride, rows_out, cols_out):
    across = jnp.zeros(padded.shape[:2] + (cols_out,), jnp.float32)
    for offset in (-1, 0, 1):
        first_col = (HALO + offset * stride).astype(jnp.int32)
        across = across + filter_taps[1, offset + 1] * lax.dynamic_slice_in_dim(padded, first_col, cols_out, 2)
    result = jnp.zeros((padded.shape[0], rows_out, cols_out), jnp.float32)
    for offset in (-1, 0, 1):
        first_row = (HALO + offset * stride).astype(jnp.int32)
        result = result + filter_taps[0, offset + 1] * lax.dynamic_slice_in_dim(across, first_row, rows_out, 1)
    return result

def filter_back(padded, filter_taps, stride, rows_out, cols_out):
    across = jnp.zeros(padded.shape[:2] + (cols_out,), jnp.float32)
    for offset in (-1, 0, 1):
        first_col = (HALO - offset * stride).astype(jnp.int32)
        across = across + filter_taps[1, offset + 1] * lax.dynamic_slice_in_dim(padded, first_col, cols_out, 2)
    result = jnp.zeros((padded.shape[0], rows_out, cols_out), jnp.float32)
    for offset in (-1, 0, 1):
        first_row = (HALO - offset * stride).astype(jnp.int32)
        result = result + filter_taps[0, offset + 1] * lax.dynamic_slice_in_dim(across, first_row, rows_out, 1)
    return result

def block_gradient(image_chan, phase_block, rows_block, weight_block, data_block):
    cos_screen = jnp.cos(phase_block)
    sin_screen = jnp.sin(phase_block)
    screened = lax.complex(cos_screen * image_chan, sin_screen * image_chan)
    spectrum = jnp.fft.fft2(screened, norm='ortho')
    picked = spectrum[rows_block]
    misfit_real = jnp.dot(jnp.real(picked), weight_block, precision=FULL_PRECISION) - data_block[0]
    misfit_imag = jnp.dot(jnp.imag(picked), weight_block, precision=FULL_PRECISION) - data_block[1]
    gridded_real = jnp.dot(misfit_real, weight_block.T, precision=FULL_PRECISION)
    gridded_imag = jnp.dot(misfit_imag, weight_block.T, precision=FULL_PRECISION)
    grid_full = jnp.zeros(spectrum.shape, spectrum.dtype).at[rows_block].add(lax.complex(gridded_real, gridded_imag))
    pulled = jnp.fft.ifft2(grid_full, norm='ortho')
    return cos_screen * jnp.real(pulled) + sin_screen * jnp.imag(pulled)

def channel_gradient(pieces):
    image_chan, phase_chan, rows_chan, weight_chan, data_chan = pieces

    def add_block(totals, block_pieces):
        phase_block, rows_block, weight_block, data_block = block_pieces
        return (totals + block_gradient(image_chan, phase_block, rows_block, weight_block, data_block), None)
    totals, unused = lax.scan(add_block, jnp.zeros_like(image_chan), (phase_chan, rows_chan, weight_chan, data_chan))
    return totals

def analyse(field, filters, spacing):
    padded = jnp.pad(field, ((0, 0), (HALO, HALO), (HALO, HALO)))
    return jnp.stack([filter_forward(padded, filters[basis_index], spacing[basis_index], field.shape[1], field.shape[2]) for basis_index in range(NBASIS)])

def synthesise(coefs, filters, spacing):
    padded = jnp.pad(coefs, ((0, 0), (0, 0), (HALO, HALO), (HALO, HALO)))
    totals = jnp.zeros(coefs.shape[1:], jnp.float32)
    for basis_index in range(NBASIS):
        totals = totals + filter_back(padded[basis_index], filters[basis_index], spacing[basis_index], coefs.shape[2], coefs.shape[3])
    return totals

def reference(sky_image, dual_coefs, phase_screen, grid_rows, grid_weight, visibilities, filters, level_counts, radius):
    spacing = lax.shift_left(jnp.ones_like(level_counts), level_counts - 1)
    radius_cells = radius[:, None, None, None]
    current = sky_image
    dual_now = dual_coefs
    for sweep_index in range(ITERS):
        gradient = lax.map(channel_gradient, (current, phase_screen, grid_rows, grid_weight, visibilities))
        synthesised = synthesise(dual_now, filters, spacing)
        updated = jnp.maximum(current - STEP_PRIMAL * (gradient + synthesised), 0.0)
        leading = 2.0 * updated - current
        raised = dual_now + STEP_DUAL * analyse(leading, filters, spacing)
        norm_cells = jnp.sqrt(lax.optimization_barrier(jnp.sum(raised * raised, axis=1, keepdims=True)))
        dual_now = raised * radius_cells / jnp.maximum(norm_cells, radius_cells)
        current = updated
    return (current, dual_now)
```

```python
import functools
import math

import jax
import jax.numpy as jnp
import ml_dtypes
import numpy as np
from jax import lax
from jax.experimental import pallas as pl
from jax.experimental.pallas import tpu as pltpu
from jax.sharding import Mesh
from jax.sharding import PartitionSpec as P

NBASIS = 9
HALO = 4
F32 = jnp.float32
BF16 = jnp.bfloat16
CHIPS = ("y", "x")
STEPS = (1, 2, 4)
SHIFTS = (0, -1, 1, -2, 2, -4, 4)
MIB = 1024 * 1024
SMEM = pl.BlockSpec(memory_space=pltpu.SMEM)
VMEM = pl.BlockSpec(memory_space=pltpu.VMEM)


def params(grid_dims=0):
    if grid_dims:
        return pltpu.CompilerParams(
            vmem_limit_bytes=48 * MIB, dimension_semantics=("arbitrary",) * grid_dims
        )
    return pltpu.CompilerParams(vmem_limit_bytes=48 * MIB)


def parts(value):
    high = value.astype(BF16)
    return high, (value - high.astype(F32)).astype(BF16)


def dot(left, right):
    return jnp.dot(left, right, preferred_element_type=F32)


def dot_t(left, right):
    return lax.dot_general(left, right, (((1,), (1,)), ((), ())), preferred_element_type=F32)


def sincos(angle):
    y = 0.5 * angle
    z = y * y
    s = F32(2.6050929582509915e-06)
    for a in (-0.00019809011067269285, 0.008333050086782038, -0.16666657944392363, 0.9999999956966753):
        s = s * z + F32(a)
    s = s * y
    c = F32(-2.6050510628158867e-07)
    for a in (
        2.476010151557824e-05,
        -0.0013888360127752544,
        0.041666636147634536,
        -0.4999999935511792,
        0.9999999997790222,
    ):
        c = c * z + F32(a)
    return 2.0 * s * c, 1.0 - 2.0 * s * s


def screens_kernel(own_ref, other_ref, cos_ref, sin_ref):
    for b, ref in enumerate((own_ref, other_ref)):
        s, c = sincos(ref[...])
        cos_ref[b] = c
        sin_ref[b] = s


def screens(own, other):
    rows, cols = own.shape
    tile = 64
    return pl.pallas_call(
        screens_kernel,
        grid=(rows // tile,),
        in_specs=[pl.BlockSpec((tile, cols), lambda i: (i, 0))] * 2,
        out_specs=[pl.BlockSpec((2, tile, cols), lambda i: (0, i, 0))] * 2,
        out_shape=[jax.ShapeDtypeStruct((2, rows, cols), F32)] * 2,
        compiler_params=params(1),
        name="screens",
    )(own, other)


def tables_kernel(gcol_ref, grow_ref, left_ref, right_ref):
    size = 512
    for b in range(2):
        for turned, g_ref, out_ref in ((0, gcol_ref, left_ref), (1, grow_ref, right_ref)):
            shape = (size, 128) if turned else (128, size)
            n = lax.broadcasted_iota(jnp.int32, shape, 0 if turned else 1)
            picked = lax.broadcasted_iota(jnp.int32, shape, 1 if turned else 0)
            index = (g_ref[b] * n) & (size - 1)
            index = jnp.where(index >= size // 2, index - size, index)
            s, c = sincos(index.astype(F32) * F32(2.0 * math.pi / size))
            high, low = parts(jnp.where(picked < 64, c, -s) * F32(1.0 / math.sqrt(size)))
            if turned:
                out_ref[b, :, :128] = high
                out_ref[b, :, 128:] = low
            else:
                out_ref[b, :128, :] = high
                out_ref[b, 128:, :] = low


def tables(rows_both):
    doubled = jnp.concatenate([rows_both, rows_both], axis=1)
    return pl.pallas_call(
        tables_kernel,
        in_specs=[VMEM, VMEM],
        out_specs=[VMEM, VMEM],
        out_shape=[
            jax.ShapeDtypeStruct((2, 256, 512), BF16),
            jax.ShapeDtypeStruct((2, 512, 256), BF16),
        ],
        compiler_params=params(),
        name="tables",
    )(doubled[:, :, None], doubled[:, None, :])


def gridding_kernel(place_ref, own_ref, other_ref, table_ref, out_ref):
    half = place_ref[0]
    odd = lax.broadcasted_iota(jnp.int32, own_ref.shape, 0) & half
    sign = jnp.where(odd == 1, F32(-1.0), F32(1.0))
    for b, ref in enumerate((own_ref, other_ref)):
        high, low = parts(ref[...] * sign)
        for part in range(2):
            value = dot(table_ref[part, 0], high)
            value = value + dot(table_ref[part, 0], low)
            value = value + dot(table_ref[part, 1], high)
            out_ref[b, part, 0], out_ref[b, part, 1] = parts(value)


def column_table():
    angle = (np.arange(512)[:, None] * np.arange(1024)[None, :] % 1024) * (2.0 * np.pi / 1024)
    out = np.zeros((2, 2, 512, 1024), ml_dtypes.bfloat16)
    for part, value in enumerate((np.cos(angle) / 32.0, -np.sin(angle) / 32.0)):
        high = value.astype(ml_dtypes.bfloat16)
        out[part, 0] = high
        out[part, 1] = (value - high.astype(np.float64)).astype(ml_dtypes.bfloat16)
    return out


def gridding(place, own, other):
    return pl.pallas_call(
        gridding_kernel,
        in_specs=[SMEM, VMEM, VMEM, VMEM],
        out_specs=VMEM,
        out_shape=jax.ShapeDtypeStruct((2, 2, 2, 512, 256), BF16),
        compiler_params=params(),
        name="gridding",
    )(place, own, other, column_table())


def thrice(left, high, low, form):
    count = left.shape[0] // 2
    both = form(left, high)
    return both[:count] + both[count:] + form(left[:count], low)


def forward_kernel(image_ref, cos_ref, sin_ref, left_ref, grid_ref, out_ref):
    image = image_ref[...]
    left = left_ref[0]
    from_real = thrice(left, *parts(cos_ref[0] * image), dot)
    from_imag = thrice(left, *parts(sin_ref[0] * image), dot)
    spectrum = jnp.concatenate(
        [from_real[:64] - from_imag[64:], from_imag[:64] + from_real[64:]], axis=0
    )
    spectrum = jnp.concatenate(parts(spectrum), axis=0)
    by_real = thrice(spectrum, grid_ref[0, 0, 0], grid_ref[0, 0, 1], dot)
    by_imag = thrice(spectrum, grid_ref[0, 1, 0], grid_ref[0, 1, 1], dot)
    seen = jnp.concatenate([by_real[:64] - by_imag[64:], by_imag[:64] + by_real[64:]], axis=0)

    @pl.when(pl.program_id(1) == 0)
    def first():
        out_ref[0] = seen

    @pl.when(pl.program_id(1) != 0)
    def later():
        out_ref[0] += seen


def forward(image, cos, sin, left, grid):
    tile = 256
    return pl.pallas_call(
        forward_kernel,
        grid=(2, 512 // tile),
        in_specs=[
            pl.BlockSpec((512, tile), lambda b, c: (0, c)),
            pl.BlockSpec((1, 512, tile), lambda b, c: (b, 0, c)),
            pl.BlockSpec((1, 512, tile), lambda b, c: (b, 0, c)),
            pl.BlockSpec((1, 256, 512), lambda b, c: (b, 0, 0)),
            pl.BlockSpec((1, 2, 2, tile, 256), lambda b, c: (b, 0, 0, c, 0)),
        ],
        out_specs=pl.BlockSpec((1, 128, 256), lambda b, c: (b, 0, 0)),
        out_shape=jax.ShapeDtypeStruct((2, 128, 256), F32),
        compiler_params=params(2),
        name="forward",
    )(image, cos, sin, left, grid)


def backward_kernel(place_ref, mine_ref, theirs_ref, data_ref, grid_ref, right_ref, cos_ref, sin_ref, *rest):
    extra_ref = rest[0] if len(rest) == 3 else None
    out_ref, total_ref = rest[-2:]
    tile = total_ref.shape[1]
    total = None
    for b in range(2):
        misfit = mine_ref[b] + theirs_ref[1 - b] - data_ref[b]
        misfit = jnp.concatenate(parts(misfit), axis=0)
        by_real = thrice(misfit, grid_ref[b, 0, 0], grid_ref[b, 0, 1], dot_t)
        by_imag = thrice(misfit, grid_ref[b, 1, 0], grid_ref[b, 1, 1], dot_t)
        real = by_real[:64] + by_imag[64:]
        imag = by_real[64:] - by_imag[:64]
        spread = jnp.concatenate(
            [jnp.concatenate([real, imag], axis=1), jnp.concatenate([imag, -real], axis=1)], axis=0
        )
        high, low = parts(spread)
        right = right_ref[b]
        pulled = dot(right, jnp.concatenate([high, high], axis=0)) + dot(right[:, :128], low)
        part = cos_ref[b] * pulled[:, :tile] + sin_ref[b] * pulled[:, tile:]
        total = part if total is None else total + part
    total_ref[0:8] = jnp.zeros((8, tile), F32)
    total_ref[520:528] = jnp.zeros((8, tile), F32)
    total_ref[8:520] = total
    for chip in range(8):
        out_ref[chip] = total_ref[64 * chip + 4 : 64 * chip + 76]
    if extra_ref is not None:
        chip = place_ref[1]
        out_ref[chip] += extra_ref[...]

        @pl.when(chip > 0)
        def above():
            out_ref[chip - 1, 64:72] += extra_ref[0:8]

        @pl.when(chip < 7)
        def below():
            out_ref[chip + 1, 0:8] += extra_ref[64:72]


def backward(place, mine, theirs, data, grid, right, cos, sin, extra=None):
    tile = 256
    seen = pl.BlockSpec((2, 128, 256), lambda c: (0, 0, 0))
    screen = pl.BlockSpec((2, 512, tile), lambda c: (0, 0, c))
    specs = [
        SMEM,
        seen,
        seen,
        seen,
        pl.BlockSpec((2, 2, 2, tile, 256), lambda c: (0, 0, 0, c, 0)),
        pl.BlockSpec((2, 512, 256), lambda c: (0, 0, 0)),
        screen,
        screen,
    ]
    args = [place, mine, theirs, data, grid, right, cos, sin]
    if extra is not None:
        specs.append(pl.BlockSpec((72, tile), lambda c: (0, c)))
        args.append(extra)
    return pl.pallas_call(
        backward_kernel,
        grid=(512 // tile,),
        in_specs=specs,
        out_specs=pl.BlockSpec((8, 72, tile), lambda c: (0, 0, c)),
        out_shape=jax.ShapeDtypeStruct((8, 72, 512), F32),
        scratch_shapes=[pltpu.VMEM((528, tile), F32)],
        compiler_params=params(1),
        name="backward",
    )(*args)


def update_kernel(place_ref, sent_ref, image_ref, own_ref, other_ref, many_ref, scratch_ref):
    half, chip = place_ref[0], place_ref[1]
    total = sent_ref[0]
    for source in range(1, 8):
        total = total + sent_ref[source]
    row = lax.broadcasted_iota(jnp.int32, total.shape, 0) + (64 * chip - HALO)
    value = jnp.maximum(image_ref[...] - 0.5 * total, 0.0)
    scratch_ref[...] = jnp.where((row >= 0) & (row < 512), value, 0.0)
    own_ref[...] = scratch_ref[pl.ds(pl.multiple_of(32 * half, 32), 40)]
    other_ref[...] = scratch_ref[pl.ds(pl.multiple_of(32 - 32 * half, 32), 40)]
    core = scratch_ref[HALO : HALO + 64]
    for target in range(8):
        many_ref[target] = core


def update(place, sent, image):
    window = jax.ShapeDtypeStruct((40, 512), F32)
    return pl.pallas_call(
        update_kernel,
        in_specs=[SMEM, VMEM, VMEM],
        out_specs=[VMEM] * 3,
        out_shape=[window, window, jax.ShapeDtypeStruct((8, 64, 512), F32)],
        scratch_shapes=[pltpu.VMEM((72, 512), F32)],
        compiler_params=params(),
        name="update",
    )(place, sent, image)


def total_kernel(place_ref, sent_ref, own_ref, other_ref, scratch_ref):
    half = place_ref[0]
    total = sent_ref[0]
    for source in range(1, 8):
        total = total + sent_ref[source]
    scratch_ref[...] = total
    own_ref[...] = scratch_ref[pl.ds(pl.multiple_of(32 * half, 32), 40)]
    other_ref[...] = scratch_ref[pl.ds(pl.multiple_of(32 - 32 * half, 32), 40)]


def total_windows(place, sent):
    window = jax.ShapeDtypeStruct((40, 512), F32)
    return pl.pallas_call(
        total_kernel,
        in_specs=[SMEM, VMEM],
        out_specs=[VMEM] * 2,
        out_shape=[window, window],
        scratch_shapes=[pltpu.VMEM((72, 512), F32)],
        compiler_params=params(),
        name="total_windows",
    )(place, sent)


def lanes_of(shape):
    return lax.broadcasted_iota(jnp.int32, shape, len(shape) - 1)


def to_facets_kernel(place_ref, own_ref, theirs_ref, out_ref, full_ref):
    half = place_ref[0]
    full_ref[0] = jnp.zeros((40, 128), F32)
    full_ref[9] = jnp.zeros((40, 128), F32)
    for i in range(4):
        full_ref[1 + 4 * half + i] = own_ref[:, 128 * i : 128 * i + 128]
        full_ref[5 - 4 * half + i] = theirs_ref[:, 128 * i : 128 * i + 128]
    lane = lanes_of((40, 128))
    for facet in range(8):
        out_ref[facet, :40] = full_ref[facet + 1]
        out_ref[facet, 40:] = jnp.where(
            lane < HALO,
            full_ref[facet + 2],
            jnp.where(lane >= 128 - HALO, full_ref[facet], 0.0),
        )


def to_facets(place, own, other):
    theirs = swapped(other)
    packed = pl.pallas_call(
        to_facets_kernel,
        in_specs=[SMEM, VMEM, VMEM],
        out_specs=VMEM,
        out_shape=jax.ShapeDtypeStruct((8, 80, 128), F32),
        scratch_shapes=[pltpu.VMEM((10, 40, 128), F32)],
        compiler_params=params(),
        name="to_facets",
    )(place, own, theirs)
    return lax.all_to_all(packed, "chan", 0, 0, tiled=True)


def to_strip_kernel(place_ref, sent_ref, own_ref, other_ref, full_ref):
    half = place_ref[0]
    lane = lanes_of((40, 128))
    for facet in range(8):
        value = sent_ref[facet, :40]
        if facet > 0:
            value = value + jnp.where(lane < HALO, sent_ref[facet - 1, 40:], 0.0)
        if facet < 7:
            value = value + jnp.where(lane >= 128 - HALO, sent_ref[facet + 1, 40:], 0.0)
        full_ref[facet] = value
    for i in range(4):
        own_ref[i] = full_ref[4 * half + i]
        other_ref[i] = full_ref[4 - 4 * half + i]


def join_kernel(place_ref, own_ref, theirs_ref, out_ref):
    half = place_ref[0]
    out_ref[...] = jnp.zeros((72, 512), F32)
    for ref, start in ((own_ref, 32 * half), (theirs_ref, 32 - 32 * half)):
        rows = pl.ds(pl.multiple_of(start, 32), 40)
        for i in range(4):
            out_ref[rows, 128 * i : 128 * i + 128] += ref[i]


def to_strip(place, partial):
    sent = lax.all_to_all(partial, "chan", 0, 0, tiled=True)
    piece = jax.ShapeDtypeStruct((4, 40, 128), F32)
    own, other = pl.pallas_call(
        to_strip_kernel,
        in_specs=[SMEM, VMEM],
        out_specs=[VMEM] * 2,
        out_shape=[piece, piece],
        scratch_shapes=[pltpu.VMEM((8, 40, 128), F32)],
        compiler_params=params(),
        name="to_strip",
    )(place, sent)
    return pl.pallas_call(
        join_kernel,
        in_specs=[SMEM, VMEM, VMEM],
        out_specs=VMEM,
        out_shape=jax.ShapeDtypeStruct((72, 512), F32),
        compiler_params=params(),
        name="join",
    )(place, own, swapped(other))


def synthesis_of(coef_ref, dual_ref, out_ref, rows_ref):
    lane = lanes_of((40, 128))

    @pl.loop(0, 8)
    def channel(ch):
        for d in range(7):
            rows_ref[d] = jnp.zeros((40, 128), F32)
        fields = [dual_ref[q, ch] for q in range(NBASIS)]

        def add(row, col, weight):
            value = weight(0) * fields[0]
            for q in range(1, NBASIS):
                value = value + weight(q) * fields[q]
            rows_ref[SHIFTS.index(col), HALO + row : HALO + row + 32] += value

        add(0, 0, lambda q: coef_ref[q, 4] + coef_ref[q, 13] + coef_ref[q, 22])
        for level, step in enumerate(STEPS):
            for a in (-1, 0, 1):
                for e in (-1, 0, 1):
                    if a or e:
                        place = 9 * level + 3 * (a + 1) + e + 1
                        add(a * step, e * step, lambda q, place=place: coef_ref[q, place])
        main = rows_ref[0]
        edge = jnp.zeros((40, 128), F32)
        for d, col in enumerate(SHIFTS):
            if col:
                turned = pltpu.roll(rows_ref[d], col % 128, 1)
                inside = (lane >= col) if col > 0 else (lane < 128 + col)
                main = main + jnp.where(inside, turned, 0.0)
                edge = edge + jnp.where(inside, 0.0, turned)
        out_ref[ch, :40] = main
        out_ref[ch, 40:] = edge


def shifted_columns(field_ref, turned_ref):
    lane = lanes_of((40, 128))

    @pl.loop(0, 8)
    def channel(ch):
        main = field_ref[ch, :40]
        edge = field_ref[ch, 40:]
        for d, col in enumerate(SHIFTS):
            if col:
                inside = (lane < 128 - col) if col > 0 else (lane >= -col)
                turned_ref[d, ch] = jnp.where(
                    inside, pltpu.roll(main, -col % 128, 1), pltpu.roll(edge, -col % 128, 1)
                )
            else:
                turned_ref[d, ch] = main


def shrink_all(taps_ref, level_ref, radius_ref, dual_ref, turned_ref, out_ref):
    @pl.loop(0, NBASIS)
    def basis(q):
        for level, step in enumerate(STEPS):

            @pl.when(level_ref[q] == level + 1)
            def at_level():
                low, mid, high = (SHIFTS.index(s) for s in (-step, 0, step))
                squares = jnp.zeros((32, 128), F32)
                for ch in range(8):
                    across = (
                        taps_ref[q, 3] * turned_ref[low, ch]
                        + taps_ref[q, 4] * turned_ref[mid, ch]
                        + taps_ref[q, 5] * turned_ref[high, ch]
                    )
                    value = (
                        taps_ref[q, 0] * across[HALO - step : HALO - step + 32]
                        + taps_ref[q, 1] * across[HALO : HALO + 32]
                        + taps_ref[q, 2] * across[HALO + step : HALO + step + 32]
                    )
                    raised = dual_ref[q, ch] + 0.5 * value
                    out_ref[q, ch] = raised
                    squares = squares + raised * raised
                limit = radius_ref[q]
                scale = limit / jnp.maximum(jnp.sqrt(squares), limit)
                for ch in range(8):
                    out_ref[q, ch] = out_ref[q, ch] * scale


def synthesis_kernel(coef_ref, dual_ref, out_ref, rows_ref):
    synthesis_of(coef_ref, dual_ref, out_ref, rows_ref)


ROWS = pltpu.VMEM((7, 40, 128), F32)
TURNED = pltpu.VMEM((7, 8, 40, 128), F32)
FIELD = pltpu.VMEM((8, 80, 128), F32)


def synthesis(coef, dual):
    return pl.pallas_call(
        synthesis_kernel,
        in_specs=[SMEM, VMEM],
        out_specs=VMEM,
        out_shape=jax.ShapeDtypeStruct((8, 80, 128), F32),
        scratch_shapes=[ROWS],
        compiler_params=params(),
        name="synthesis",
    )(coef, dual)


def middle_kernel(coef_ref, taps_ref, level_ref, radius_ref, dual_ref, before_ref, now_ref,
                  dual_out, part_out, right_out, left_out, field_ref, turned_ref, rows_ref):
    field_ref[...] = 2.0 * now_ref[...] - before_ref[...]
    shifted_columns(field_ref, turned_ref)
    shrink_all(taps_ref, level_ref, radius_ref, dual_ref, turned_ref, dual_out)
    synthesis_of(coef_ref, dual_out, part_out, rows_ref)
    lane = lanes_of((40, 128))
    for ch in range(8):
        main, edge = part_out[ch, :40], part_out[ch, 40:]
        right_out[ch] = jnp.where(lane >= 128 - HALO, main, edge)
        left_out[ch] = jnp.where(lane < HALO, main, edge)


def middle(coef, taps, levels, radius, dual, before, now):
    side = jax.ShapeDtypeStruct((8, 40, 128), F32)
    return pl.pallas_call(
        middle_kernel,
        in_specs=[SMEM] * 4 + [VMEM] * 3,
        out_specs=[VMEM] * 4,
        out_shape=[
            jax.ShapeDtypeStruct((NBASIS, 8, 32, 128), F32),
            jax.ShapeDtypeStruct((8, 80, 128), F32),
            side,
            side,
        ],
        scratch_shapes=[FIELD, TURNED, ROWS],
        compiler_params=params(),
        name="middle",
    )(coef, taps, levels, radius, dual, before, now)


def last_kernel(place_ref, taps_ref, level_ref, radius_ref, dual_ref, now_ref, part_ref, above_ref,
                below_ref, gradient_ref, image_out, dual_out, field_ref, turned_ref):
    chip_row, facet = place_ref[2], place_ref[3]
    lane = lanes_of((40, 128))
    row = lax.broadcasted_iota(jnp.int32, (40, 128), 0) + (32 * chip_row - HALO)
    in_rows = (row >= 0) & (row < 512)
    in_edge = ((lane < HALO) & (facet < 7)) | ((lane >= 128 - HALO) & (facet > 0))
    for ch in range(8):
        for start, keep in ((0, in_rows), (40, in_rows & in_edge)):
            which = start // 40
            field_ref[ch, start : start + 40] = (
                part_ref[ch, start : start + 40] + gradient_ref[ch, start : start + 40]
            )
            field_ref[ch, start : start + 8] += above_ref[ch, which]
            field_ref[ch, start + 32 : start + 40] += below_ref[ch, which]
            now = now_ref[ch, start : start + 40]
            value = jnp.maximum(now - 0.5 * field_ref[ch, start : start + 40], 0.0)
            value = jnp.where(keep, value, 0.0)
            if start == 0:
                image_out[ch] = value[HALO : HALO + 32]
            field_ref[ch, start : start + 40] = 2.0 * value - now
    shifted_columns(field_ref, turned_ref)
    shrink_all(taps_ref, level_ref, radius_ref, dual_ref, turned_ref, dual_out)


def last(place, taps, levels, radius, dual, now, part, above, below, gradient):
    return pl.pallas_call(
        last_kernel,
        in_specs=[SMEM] * 4 + [VMEM] * 6,
        out_specs=[VMEM] * 2,
        out_shape=[
            jax.ShapeDtypeStruct((8, 32, 128), F32),
            jax.ShapeDtypeStruct((NBASIS, 8, 32, 128), F32),
        ],
        scratch_shapes=[FIELD, TURNED],
        compiler_params=params(),
        name="last",
    )(place, taps, levels, radius, dual, now, part, above, below, gradient)


def swapped(value):
    return lax.ppermute(value, "core", [(0, 1), (1, 0)])


def neighbours(value, axis, count, step):
    return lax.ppermute(
        value, axis, [(i, i + step) for i in range(count) if 0 <= i + step < count]
    )


def half_of(value, half, size, dim):
    return lax.dynamic_slice_in_dim(value, half * size, size, dim)


def per_device(
    sky_image,
    dual_coefs,
    phase_screen,
    grid_rows,
    grid_weight,
    visibilities,
    filters,
    level_counts,
    radius,
):
    half = lax.axis_index("core")
    chip = lax.axis_index("y") * 4 + lax.axis_index("x")
    facet = lax.axis_index("chan")
    place = jnp.stack([half, chip, chip * 2 + half, facet]).astype(jnp.int32)
    taps = filters.reshape(NBASIS, 6)
    outer = (filters[:, 0, :, None] * filters[:, 1, None, :]).reshape(NBASIS, 1, 9)
    is_level = (level_counts[:, None] == jnp.arange(1, 4)[None, :]).astype(F32)
    coef = (is_level[:, :, None] * outer).reshape(NBASIS, 27)

    strip = lax.all_to_all(sky_image, "chan", 0, 0, tiled=True)
    own = half_of(strip, half, 4, 0)
    theirs = swapped(half_of(strip, 1 - half, 4, 0))
    first = jnp.where(half == 0, own, theirs)
    second = jnp.where(half == 0, theirs, own)
    strip = jnp.stack([first, second]).transpose(0, 2, 1, 3).reshape(64, 512)
    image = lax.all_to_all(
        jnp.broadcast_to(strip[None], (8, 64, 512)), CHIPS, 0, 0, tiled=True
    ).reshape(512, 512)

    phase = phase_screen[0, 0]
    phase_own = half_of(phase, half, 512, 1)
    phase_other = swapped(half_of(phase, 1 - half, 512, 1))
    weight_own = grid_weight[0, 0]
    weight_other = swapped(weight_own)
    data_own = visibilities[0, 0].reshape(128, 256)
    data_both = jnp.stack([data_own, swapped(data_own)])
    rows_own = grid_rows[0, 0]
    rows_other = swapped(rows_own.astype(F32)).astype(jnp.int32)
    left, right = tables(jnp.stack([rows_own, rows_other]))
    cos, sin = screens(phase_own, phase_other)
    grid = gridding(place, weight_own, weight_other)

    extra = to_strip(place, synthesis(coef, dual_coefs))
    seen = forward(image, cos, sin, left, grid)
    window = lax.dynamic_slice_in_dim(jnp.pad(image, ((HALO, HALO), (0, 0))), 64 * chip, 72, 0)
    before = to_facets(
        place, half_of_rows(window, half), half_of_rows(window, 1 - half)
    )
    sent = backward(place, seen, swapped(seen), data_both, grid, right, cos, sin, extra)
    sent = lax.all_to_all(sent, CHIPS, 0, 0, tiled=True)
    own, other, many = update(place, sent, window)

    image = lax.all_to_all(many, CHIPS, 0, 0, tiled=True).reshape(512, 512)
    now = to_facets(place, own, other)
    seen = forward(image, cos, sin, left, grid)
    dual, part, to_right, to_left = middle(
        coef, taps, level_counts, radius, dual_coefs, before, now
    )
    sent = backward(place, seen, swapped(seen), data_both, grid, right, cos, sin)
    sent = lax.all_to_all(sent, CHIPS, 0, 0, tiled=True)
    from_left = neighbours(to_right, "chan", 8, 1)
    from_right = neighbours(to_left, "chan", 8, -1)
    lane = lanes_of((8, 40, 128))
    main = part[:, :40] + jnp.where(lane < HALO, from_left, 0.0)
    main = main + jnp.where(lane >= 128 - HALO, from_right, 0.0)
    edge = part[:, 40:] + jnp.where(lane >= 128 - HALO, from_left, 0.0)
    edge = edge + jnp.where(lane < HALO, from_right, 0.0)
    both = jnp.stack([main, edge], axis=1)
    above = neighbours(both[:, :, 32:], ("y", "x", "core"), 16, 1)
    below = neighbours(both[:, :, :8], ("y", "x", "core"), 16, -1)
    gradient = to_facets(place, *total_windows(place, sent))
    return tuple(
        last(
            place, taps, level_counts, radius, dual, now, both.reshape(8, 80, 128), above, below, gradient
        )
    )


def half_of_rows(window, half):
    return lax.dynamic_slice_in_dim(window, 32 * half, 40, 0)


def solution(mesh):
    fine = Mesh(mesh.devices.reshape(8, 2, 4, 2), ("chan", "y", "x", "core"))
    rows = ("y", "x", "core")
    placed = (
        P(None, rows, "chan"),
        P(None, None, rows, "chan"),
        P("chan", rows, None, None),
        P("chan", rows, None),
        P("chan", rows, None, None),
        P("chan", rows, None, None, None),
        P(),
        P(),
        P(),
    )
    return jax.shard_map(
        per_device,
        mesh=fine,
        in_specs=placed,
        out_specs=(P(None, rows, "chan"), P(None, None, rows, "chan")),
        check_vma=False,
    )
```

```python
import functools
import math

import jax
import jax.numpy as jnp
import ml_dtypes
import numpy as np
from jax import lax
from jax.experimental import pallas as pl
from jax.experimental.pallas import tpu as pltpu
from jax.sharding import Mesh
from jax.sharding import PartitionSpec as P

NBASIS = 9
HALO = 4
F32 = jnp.float32
BF16 = jnp.bfloat16
CHIPS = ("y", "x")
STEPS = (1, 2, 4)
SHIFTS = (0, -1, 1, -2, 2, -4, 4)
MIB = 1024 * 1024
SMEM = pl.BlockSpec(memory_space=pltpu.SMEM)
VMEM = pl.BlockSpec(memory_space=pltpu.VMEM)
ANY = pl.BlockSpec(memory_space=pltpu.HBM)


def params(size=16):
    return pltpu.CompilerParams(vmem_limit_bytes=size * MIB)


def where_am_i():
    half = lax.axis_index("core")
    chip = lax.axis_index("y") * 4 + lax.axis_index("x")
    return half, chip, 2 * chip + half, lax.axis_index("chan")


def cost(us):
    return pl.CostEstimate(flops=0, bytes_accessed=int(us * 3.0e6), transcendentals=0)


def sent_out(*shape):
    return pltpu.HBM(shape, F32)


def kept(shape, kind=F32):
    return pltpu.VMEM(shape, kind)


def in_hbm(value):
    return pltpu.with_memory_space_constraint(value, pltpu.HBM)


def parts(value):
    high = value.astype(BF16)
    return high, (value - high.astype(F32)).astype(BF16)


def dot(left, right):
    return jnp.dot(left, right, preferred_element_type=F32)


def dot_t(left, right):
    return lax.dot_general(left, right, (((1,), (1,)), ((), ())), preferred_element_type=F32)


def sincos(angle):
    y = 0.5 * angle
    z = y * y
    s = F32(2.6050929582509915e-06)
    for a in (-0.00019809011067269285, 0.008333050086782038, -0.16666657944392363, 0.9999999956966753):
        s = s * z + F32(a)
    s = s * y
    c = F32(-2.6050510628158867e-07)
    for a in (
        2.476010151557824e-05,
        -0.0013888360127752544,
        0.041666636147634536,
        -0.4999999935511792,
        0.9999999997790222,
    ):
        c = c * z + F32(a)
    return 2.0 * s * c, 1.0 - 2.0 * s * s


def rounded(value):
    return ((value * 32767.0 + 32768.5).astype(jnp.int32) - 32768).astype(jnp.int16)


def widened(value):
    return value.astype(jnp.int32).astype(F32)


def screens_kernel(other_ref, phase_hbm, out_ref, own_ref, sems):
    cols = pl.ds(pl.multiple_of(512 * lax.axis_index("core"), 512), 512)
    copies = [
        pltpu.make_async_copy(
            phase_hbm.at[pl.ds(128 * i, 128), cols], own_ref.at[pl.ds(128 * i, 128)], sems.at[i]
        )
        for i in range(4)
    ]
    for copy in copies:
        copy.start()

    def fill(b, ref, start):
        at = pl.ds(pl.multiple_of(start, 32), 32)
        s, c = sincos(ref[at])
        for part in range(2):
            cols = slice(256 * part, 256 * part + 256)
            out_ref[b, part, 0, at] = rounded(c[:, cols])
            out_ref[b, part, 1, at] = rounded(s[:, cols])

    pl.loop(0, 512, step=32)(functools.partial(fill, 1, other_ref))
    for i in range(4):
        copies[i].wait()
        pl.loop(128 * i, 128 * i + 128, step=32)(functools.partial(fill, 0, own_ref))


def screens(phase, other):
    return pl.pallas_call(
        screens_kernel,
        in_specs=[VMEM, ANY],
        out_specs=VMEM,
        out_shape=kept((2, 2, 2, 512, 256), jnp.int16),
        scratch_shapes=[pltpu.VMEM((512, 512), F32), pltpu.SemaphoreType.DMA((4,))],
        compiler_params=params(),
        cost_estimate=cost(4),
        name="screens",
    )(other, in_hbm(phase))


def tables_kernel(gcol_ref, grow_ref, left_ref, right_ref):
    size = 512
    for b in range(2):
        for turned, g_ref, out_ref in ((0, gcol_ref, left_ref), (1, grow_ref, right_ref)):
            shape = (size, 128) if turned else (128, size)
            n = lax.broadcasted_iota(jnp.int32, shape, 0 if turned else 1)
            picked = lax.broadcasted_iota(jnp.int32, shape, 1 if turned else 0)
            index = (g_ref[b] * n) & (size - 1)
            index = jnp.where(index >= size // 2, index - size, index)
            s, c = sincos(index.astype(F32) * F32(2.0 * math.pi / size))
            high, low = parts(jnp.where(picked < 64, c, -s) * F32(1.0 / math.sqrt(size)))
            if turned:
                out_ref[b, :, :128] = high
                out_ref[b, :, 128:] = low
            else:
                out_ref[b, :128, :] = high
                out_ref[b, 128:, :] = low


def tables(rows_both):
    doubled = jnp.concatenate([rows_both, rows_both], axis=1)
    return pl.pallas_call(
        tables_kernel,
        in_specs=[VMEM, VMEM],
        out_specs=[VMEM, VMEM],
        out_shape=[
            pltpu.HBM((2, 256, 512), BF16),
            pltpu.HBM((2, 512, 256), BF16),
        ],
        compiler_params=params(),
        cost_estimate=cost(2),
        name="tables",
    )(doubled[:, :, None], doubled[:, None, :])


def gridding_kernel(own_ref, other_ref, table_ref, out_ref):
    half = lax.axis_index("core")
    odd = lax.broadcasted_iota(jnp.int32, own_ref.shape, 0) & half
    sign = jnp.where(odd == 1, F32(-1.0), F32(1.0))
    for b, ref in enumerate((own_ref, other_ref)):
        high, low = parts(ref[...] * sign)
        for part in range(2):
            value = dot(table_ref[part, 0], high)
            value = value + dot(table_ref[part, 0], low)
            value = value + dot(table_ref[part, 1], high)
            for cols in range(2):
                kept_high, kept_low = parts(value[256 * cols : 256 * cols + 256])
                out_ref[b, cols, part, 0] = kept_high
                out_ref[b, cols, part, 1] = kept_low


def column_table():
    angle = (np.arange(512)[:, None] * np.arange(1024)[None, :] % 1024) * (2.0 * np.pi / 1024)
    out = np.zeros((2, 2, 512, 1024), ml_dtypes.bfloat16)
    for part, value in enumerate((np.cos(angle) / 32.0, -np.sin(angle) / 32.0)):
        high = value.astype(ml_dtypes.bfloat16)
        out[part, 0] = high
        out[part, 1] = (value - high.astype(np.float64)).astype(ml_dtypes.bfloat16)
    return out


def gridding(own, other):
    return pl.pallas_call(
        gridding_kernel,
        in_specs=[VMEM, VMEM, VMEM],
        out_specs=VMEM,
        out_shape=pltpu.HBM((2, 2, 2, 2, 256, 256), BF16),
        compiler_params=params(),
        cost_estimate=cost(7),
        name="gridding",
    )(own, other, column_table())


def thrice(left, high, low, form):
    count = left.shape[0] // 2
    both = form(left, high)
    return both[:count] + both[count:] + form(left[:count], low)


def fetch(table_hbm, grid_hbm, table_ref, grid_ref, sems, order):
    copies = {}
    for i, key in enumerate(order):
        source, target = (table_hbm, table_ref) if len(key) == 1 else (grid_hbm, grid_ref)
        copies[key] = pltpu.make_async_copy(source.at[key], target.at[key], sems.at[i])
        copies[key].start()
    return copies


FETCHED = [
    pltpu.VMEM((2, 2, 2, 2, 256, 256), BF16),
    pltpu.SemaphoreType.DMA((6,)),
]


def forward_kernel(image_ref, trig_ref, left_hbm, grid_hbm, out_ref, copy_ref, left_ref, grid_ref, sems):
    order = [(0,), (0, 0), (0, 1), (1,), (1, 0), (1, 1)]
    copies = fetch(left_hbm, grid_hbm, left_ref, grid_ref, sems, order)
    for b in range(2):
        total = None
        copies[(b,)].wait()
        left = left_ref[b]
        for part in range(2):
            image = image_ref[:, 256 * part : 256 * part + 256] * F32(1.0 / 32767.0)
            from_real = thrice(left, *parts(widened(trig_ref[b, part, 0]) * image), dot)
            from_imag = thrice(left, *parts(widened(trig_ref[b, part, 1]) * image), dot)
            spectrum = jnp.concatenate(
                [from_real[:64] - from_imag[64:], from_imag[:64] + from_real[64:]], axis=0
            )
            spectrum = jnp.concatenate(parts(spectrum), axis=0)
            copies[(b, part)].wait()
            by_real = thrice(spectrum, grid_ref[b, part, 0, 0], grid_ref[b, part, 0, 1], dot)
            by_imag = thrice(spectrum, grid_ref[b, part, 1, 0], grid_ref[b, part, 1, 1], dot)
            seen = jnp.concatenate(
                [by_real[:64] - by_imag[64:], by_imag[:64] + by_real[64:]], axis=0
            )
            total = seen if total is None else total + seen
        out_ref[b] = total
        copy_ref[b] = total


def forward(image, trig, left, grid):
    return pl.pallas_call(
        forward_kernel,
        in_specs=[VMEM, VMEM, ANY, ANY],
        out_specs=[VMEM] * 2,
        out_shape=[jax.ShapeDtypeStruct((2, 128, 256), F32)] * 2,
        scratch_shapes=[pltpu.VMEM((2, 256, 512), BF16)] + FETCHED,
        compiler_params=params(20),
        cost_estimate=cost(4),
        name="forward",
    )(image, trig, in_hbm(left), in_hbm(grid))


def backward_kernel(mine_ref, theirs_ref, data_ref, trig_ref, *rest):
    extra_ref = rest[0] if len(rest) == 8 else None
    right_hbm, grid_hbm, out_ref, total_ref, right_ref, grid_ref, sems = rest[-7:]
    order = [(0, 0), (0,), (1, 0), (1,), (0, 1), (1, 1)]
    copies = fetch(right_hbm, grid_hbm, right_ref, grid_ref, sems, order)
    total_ref[0:8] = jnp.zeros((8, 512), F32)
    total_ref[520:528] = jnp.zeros((8, 512), F32)
    misfits = [
        jnp.concatenate(parts(mine_ref[b] + theirs_ref[1 - b] - data_ref[b]), axis=0) for b in range(2)
    ]
    for half in range(2):
        cols = slice(256 * half, 256 * half + 256)
        total = None
        for b in range(2):
            copies[(b, half)].wait()
            by_real = thrice(misfits[b], grid_ref[b, half, 0, 0], grid_ref[b, half, 0, 1], dot_t)
            by_imag = thrice(misfits[b], grid_ref[b, half, 1, 0], grid_ref[b, half, 1, 1], dot_t)
            real = by_real[:64] + by_imag[64:]
            imag = by_real[64:] - by_imag[:64]
            spread = jnp.concatenate(
                [jnp.concatenate([real, imag], axis=1), jnp.concatenate([imag, -real], axis=1)],
                axis=0,
            )
            high, low = parts(spread * F32(1.0 / 32767.0))
            if half == 0:
                copies[(b,)].wait()
            right = right_ref[b]
            pulled = dot(right, jnp.concatenate([high, high], axis=0)) + dot(right[:, :128], low)
            part = widened(trig_ref[b, half, 0]) * pulled[:, :256]
            part = part + widened(trig_ref[b, half, 1]) * pulled[:, 256:]
            total = part if total is None else total + part
        total_ref[8:520, cols] = total
        for chip in range(8):
            out_ref[chip, :, cols] = total_ref[64 * chip + 4 : 64 * chip + 76, cols]
    if extra_ref is not None:
        chip = where_am_i()[1]
        out_ref[chip] += extra_ref[...]

        @pl.when(chip > 0)
        def above():
            out_ref[chip - 1, 64:72] += extra_ref[0:8]

        @pl.when(chip < 7)
        def below():
            out_ref[chip + 1, 0:8] += extra_ref[64:72]


def backward(mine, theirs, data, grid, right, trig, extra=None):
    args = [mine, theirs, data, trig] + ([] if extra is None else [extra])
    return pl.pallas_call(
        backward_kernel,
        in_specs=[VMEM] * len(args) + [ANY] * 2,
        out_specs=VMEM,
        out_shape=sent_out(8, 72, 512),
        scratch_shapes=[pltpu.VMEM((528, 512), F32), pltpu.VMEM((2, 512, 256), BF16)] + FETCHED,
        compiler_params=params(20),
        cost_estimate=cost(5),
        name="backward",
    )(*args, in_hbm(right), in_hbm(grid))


def update_kernel(sent_ref, image_ref, own_ref, other_ref, many_ref, scratch_ref):
    half, chip = where_am_i()[:2]
    total = sent_ref[0]
    for source in range(1, 8):
        total = total + sent_ref[source]
    row = lax.broadcasted_iota(jnp.int32, total.shape, 0) + (64 * chip - HALO)
    value = jnp.maximum(image_ref[...] - 0.5 * total, 0.0)
    scratch_ref[...] = jnp.where((row >= 0) & (row < 512), value, 0.0)
    for window_ref, start in ((own_ref, 32 * half), (other_ref, 32 - 32 * half)):
        rows = pl.ds(pl.multiple_of(start, 32), 40)
        window_ref[0] = scratch_ref[rows]
        window_ref[1] = image_ref[rows]
    core = scratch_ref[HALO : HALO + 64]
    for target in range(8):
        many_ref[target] = core


def update(sent, image):
    window = jax.ShapeDtypeStruct((2, 40, 512), F32)
    return pl.pallas_call(
        update_kernel,
        in_specs=[VMEM, VMEM],
        out_specs=[VMEM] * 3,
        out_shape=[window, sent_out(2, 40, 512), sent_out(8, 64, 512)],
        scratch_shapes=[pltpu.VMEM((72, 512), F32)],
        compiler_params=params(),
        cost_estimate=cost(1),
        name="update",
    )(sent, image)


def total_kernel(sent_ref, own_ref, other_ref, scratch_ref):
    half = lax.axis_index("core")
    total = sent_ref[0]
    for source in range(1, 8):
        total = total + sent_ref[source]
    scratch_ref[...] = total
    own_ref[...] = scratch_ref[pl.ds(pl.multiple_of(32 * half, 32), 40)]
    other_ref[...] = scratch_ref[pl.ds(pl.multiple_of(32 - 32 * half, 32), 40)]


def total_windows(sent):
    window = jax.ShapeDtypeStruct((40, 512), F32)
    return pl.pallas_call(
        total_kernel,
        in_specs=[VMEM],
        out_specs=[VMEM] * 2,
        out_shape=[window, sent_out(40, 512)],
        scratch_shapes=[pltpu.VMEM((72, 512), F32)],
        compiler_params=params(),
        cost_estimate=cost(1),
        name="total_windows",
    )(sent)


def lanes_of(shape):
    return lax.broadcasted_iota(jnp.int32, shape, len(shape) - 1)


def packed_edge(edge):
    lane = lanes_of((8, 128))
    out = jnp.zeros((8, 128), F32)
    for g in range(5):
        turned = pltpu.roll(edge[8 * g : 8 * g + 8], 8 * g + HALO, 1)
        out = jnp.where((lane >= 8 * g) & (lane < 8 * g + 8), turned, out)
    return out


def unpacked_edge(packed):
    lane = lanes_of((40, 128))
    turned = [pltpu.roll(packed, 128 - HALO - 8 * g, 1) for g in range(5)]
    inside = (lane < HALO) | (lane >= 128 - HALO)
    return jnp.where(inside, jnp.concatenate(turned, axis=0), 0.0)


def to_facets_kernel(own_ref, theirs_ref, out_ref, full_ref):
    half = lax.axis_index("core")
    full_ref[0] = jnp.zeros((40, 128), F32)
    full_ref[9] = jnp.zeros((40, 128), F32)
    for i in range(4):
        full_ref[1 + 4 * half + i] = own_ref[:, 128 * i : 128 * i + 128]
        full_ref[5 - 4 * half + i] = theirs_ref[:, 128 * i : 128 * i + 128]
    lane = lanes_of((40, 128))
    for facet in range(8):
        out_ref[facet, :40] = full_ref[facet + 1]
        out_ref[facet, 40:] = packed_edge(
            jnp.where(lane < HALO, full_ref[facet + 2], full_ref[facet])
        )


def to_facets(own, other):
    theirs = swapped(other)
    return pl.pallas_call(
        to_facets_kernel,
        in_specs=[VMEM, VMEM],
        out_specs=VMEM,
        out_shape=sent_out(8, 48, 128),
        scratch_shapes=[pltpu.VMEM((10, 40, 128), F32)],
        compiler_params=params(),
        cost_estimate=cost(1),
        name="to_facets",
    )(own, theirs)


def pair_kernel(own_ref, theirs_ref, out_ref, full_ref):
    half = lax.axis_index("core")
    for which in range(2):
        full_ref[which, 0] = jnp.zeros((40, 128), F32)
        full_ref[which, 9] = jnp.zeros((40, 128), F32)
        for i in range(4):
            full_ref[which, 1 + 4 * half + i] = own_ref[which, :, 128 * i : 128 * i + 128]
            full_ref[which, 5 - 4 * half + i] = theirs_ref[which, :, 128 * i : 128 * i + 128]
    lane = lanes_of((40, 128))
    row = lax.broadcasted_iota(jnp.int32, (8, 128), 0)
    for facet in range(8):
        out_ref[facet, :40] = full_ref[0, facet + 1]
        for which in range(2):
            out_ref[facet, 40 + 8 * which : 48 + 8 * which] = packed_edge(
                jnp.where(lane < HALO, full_ref[which, facet + 2], full_ref[which, facet])
            )
        out_ref[facet, 56:64] = jnp.where(
            row < HALO, full_ref[1, facet + 1, 0:8], full_ref[1, facet + 1, 32:40]
        )


def pair_to_facets(own, other):
    theirs = swapped(other)
    return pl.pallas_call(
        pair_kernel,
        in_specs=[VMEM, VMEM],
        out_specs=VMEM,
        out_shape=sent_out(8, 64, 128),
        scratch_shapes=[pltpu.VMEM((2, 10, 40, 128), F32)],
        compiler_params=params(),
        cost_estimate=cost(1),
        name="pair_to_facets",
    )(own, theirs)


def split_kernel(sent_ref, image_own, image_other, term_own, term_other, full_ref):
    half = lax.axis_index("core")
    lane = lanes_of((40, 128))
    edges = [unpacked_edge(sent_ref[facet, 72:80]) for facet in range(8)]
    for facet in range(8):
        value = sent_ref[facet, 32:72]
        if facet > 0:
            value = value + jnp.where(lane < HALO, edges[facet - 1], 0.0)
        if facet < 7:
            value = value + jnp.where(lane >= 128 - HALO, edges[facet + 1], 0.0)
        full_ref[facet] = value
    for i in range(4):
        cols = slice(128 * i, 128 * i + 128)
        image_own[:, cols] = sent_ref[4 * half + i, 0:32]
        image_other[:, cols] = sent_ref[4 - 4 * half + i, 0:32]
        term_own[:, cols] = full_ref[4 * half + i]
        term_other[:, cols] = full_ref[4 - 4 * half + i]


def split(sent):
    return pl.pallas_call(
        split_kernel,
        in_specs=[VMEM],
        out_specs=[VMEM] * 4,
        out_shape=[
            jax.ShapeDtypeStruct((32, 512), F32),
            sent_out(32, 512),
            jax.ShapeDtypeStruct((40, 512), F32),
            sent_out(40, 512),
        ],
        scratch_shapes=[pltpu.VMEM((8, 40, 128), F32)],
        compiler_params=params(),
        cost_estimate=cost(1),
        name="split",
    )(sent)


def spread_kernel(own_ref, theirs_ref, out_ref):
    half = lax.axis_index("core")
    for ref, start in ((own_ref, 32 * half), (theirs_ref, 32 - 32 * half)):
        rows = pl.ds(pl.multiple_of(start, 32), 32)
        value = ref[...]
        for target in range(8):
            out_ref[target, rows] = value


def spread(own, theirs):
    return pl.pallas_call(
        spread_kernel,
        in_specs=[VMEM, VMEM],
        out_specs=VMEM,
        out_shape=sent_out(8, 64, 512),
        compiler_params=params(),
        cost_estimate=cost(1),
        name="spread",
    )(own, theirs)


def join_kernel(own_ref, theirs_ref, out_ref):
    half = lax.axis_index("core")
    out_ref[...] = jnp.zeros((72, 512), F32)
    for ref, start in ((own_ref, 32 * half), (theirs_ref, 32 - 32 * half)):
        rows = pl.ds(pl.multiple_of(start, 32), 40)
        out_ref[rows] += ref[...]


def join(own, theirs):
    return pl.pallas_call(
        join_kernel,
        in_specs=[VMEM, VMEM],
        out_specs=VMEM,
        out_shape=jax.ShapeDtypeStruct((72, 512), F32),
        compiler_params=params(),
        cost_estimate=cost(1),
        name="join",
    )(own, theirs)


def spread_rows(scal_ref, q, step, ch, field, padded_ref, total_ref):
    padded_ref[ch, 8:40] = field
    low, mid, high = HALO + step, HALO, HALO - step
    value = (
        scal_ref[q, 0] * padded_ref[ch, low : low + 40]
        + scal_ref[q, 1] * padded_ref[ch, mid : mid + 40]
        + scal_ref[q, 2] * padded_ref[ch, high : high + 40]
    )
    for e in range(3):
        total_ref[SHIFTS.index((e - 1) * step), ch] += scal_ref[q, 3 + e] * value


def clear(padded_ref, total_ref):
    for ch in range(8):
        padded_ref[ch, 0:8] = jnp.zeros((8, 128), F32)
        padded_ref[ch, 40:48] = jnp.zeros((8, 128), F32)
        for d in range(7):
            total_ref[d, ch] = jnp.zeros((40, 128), F32)


def shift_all(total_ref, ch):
    lane = lanes_of((40, 128))
    main = total_ref[0, ch]
    edge = jnp.zeros((40, 128), F32)
    for d, col in enumerate(SHIFTS):
        if col:
            turned = pltpu.roll(total_ref[d, ch], col % 128, 1)
            inside = (lane >= col) if col > 0 else (lane < 128 + col)
            main = main + jnp.where(inside, turned, 0.0)
            edge = edge + jnp.where(inside, 0.0, turned)
    return main, edge


def shifted_columns(field_ref, turned_ref):
    lane = lanes_of((40, 128))

    @pl.loop(0, 8)
    def channel(ch):
        main = field_ref[ch, :40]
        edge = field_ref[ch, 40:]
        for d, col in enumerate(SHIFTS):
            if col:
                inside = (lane < 128 - col) if col > 0 else (lane >= -col)
                turned_ref[d, ch] = jnp.where(
                    inside, pltpu.roll(main, -col % 128, 1), pltpu.roll(edge, -col % 128, 1)
                )
            else:
                turned_ref[d, ch] = main


def each_level(scal_ref, q, work):
    for level, step in enumerate(STEPS):
        pl.when(scal_ref[q, 7] == F32(level + 1))(functools.partial(work, step))


def shrink(scal_ref, q, at, dual_ref, turned_ref, out_ref, after=None):
    def at_level(step):
        low, mid, high = (SHIFTS.index(s) for s in (-step, 0, step))
        squares = jnp.zeros((32, 128), F32)
        for ch in range(8):
            across = (
                scal_ref[q, 3] * turned_ref[low, ch]
                + scal_ref[q, 4] * turned_ref[mid, ch]
                + scal_ref[q, 5] * turned_ref[high, ch]
            )
            value = (
                scal_ref[q, 0] * across[HALO - step : HALO - step + 32]
                + scal_ref[q, 1] * across[HALO : HALO + 32]
                + scal_ref[q, 2] * across[HALO + step : HALO + step + 32]
            )
            raised = dual_ref[at, ch] + 0.5 * value
            out_ref[at, ch] = raised
            squares = squares + raised * raised
        limit = scal_ref[q, 6]
        scale = limit / jnp.maximum(jnp.sqrt(squares), limit)
        for ch in range(8):
            value = out_ref[at, ch] * scale
            out_ref[at, ch] = value
            if after is not None:
                after(step, ch, value)

    each_level(scal_ref, q, at_level)


class Scalars:
    def __init__(self, filters_ref, level_ref):
        self.filters_ref = filters_ref
        self.level_ref = level_ref

    def __getitem__(self, at):
        q, column = at
        if column == 7:
            return self.level_ref[q].astype(F32)
        return self.filters_ref[q, column // 3, column % 3]


def start_kernel(filters_ref, level_ref, image_ref, dual_ref, out_ref, padded_ref, total_ref):
    step_index = pl.program_id(0)
    scal_ref = Scalars(filters_ref, level_ref)

    @pl.when(step_index == 0)
    def first():
        clear(padded_ref, total_ref)

    @pl.loop(0, 3)
    def basis(i):
        q = 3 * step_index + i

        def at_level(step):
            for ch in range(8):
                spread_rows(scal_ref, q, step, ch, dual_ref[i, ch], padded_ref, total_ref)

        each_level(scal_ref, q, at_level)

    @pl.when(step_index == 2)
    def final():
        for ch in range(8):
            main, edge = shift_all(total_ref, ch)
            out_ref[ch, 0:32] = image_ref[ch]
            out_ref[ch, 32:72] = main
            out_ref[ch, 72:80] = packed_edge(edge)


TURNED = pltpu.VMEM((7, 8, 40, 128), F32)
FIELD = pltpu.VMEM((8, 80, 128), F32)
PADDED = pltpu.VMEM((8, 48, 128), F32)
THIRD = pl.BlockSpec((3, 8, 32, 128), lambda i: (i, 0, 0, 0))


def whole(*shape):
    return pl.BlockSpec(shape, lambda i: (0,) * len(shape))


def start(filters, levels, image, dual):
    return pl.pallas_call(
        start_kernel,
        grid=(3,),
        in_specs=[SMEM, SMEM, whole(8, 32, 128), THIRD],
        out_specs=whole(8, 80, 128),
        out_shape=sent_out(8, 80, 128),
        scratch_shapes=[PADDED, TURNED],
        compiler_params=params(),
        cost_estimate=cost(4),
        name="start",
    )(filters, levels, in_hbm(image), in_hbm(dual))


def middle_kernel(scal_ref, before_ref, pair_ref, dual_ref, dual_out, part_out, right_out, left_out,
                  now_out, field_ref, turned_ref, padded_ref, total_ref):
    step_index = pl.program_id(0)

    @pl.when(step_index == 0)
    def first():
        for ch in range(8):
            main = pair_ref[ch, :40]
            now_out[ch, :40] = main
            now = 2.0 * main
            field_ref[ch, 4:36] = now[4:36] - before_ref[ch]
            outer = pair_ref[ch, 56:64]
            field_ref[ch, 0:4] = now[0:4] - outer[0:4]
            field_ref[ch, 36:40] = now[36:40] - outer[4:8]
            edge = unpacked_edge(pair_ref[ch, 40:48])
            now_out[ch, 40:] = edge
            field_ref[ch, 40:] = 2.0 * edge - unpacked_edge(pair_ref[ch, 48:56])
        shifted_columns(field_ref, turned_ref)
        clear(padded_ref, total_ref)

    @pl.loop(0, 3)
    def basis(i):
        q = 3 * step_index + i

        def after(step, ch, value):
            spread_rows(scal_ref, q, step, ch, value, padded_ref, total_ref)

        shrink(scal_ref, q, i, dual_ref, turned_ref, dual_out, after)

    @pl.when(step_index == 2)
    def final():
        lane = lanes_of((40, 128))
        for ch in range(8):
            main, edge = shift_all(total_ref, ch)
            part_out[ch, :40] = main
            part_out[ch, 40:] = edge
            right_out[ch] = jnp.where(lane >= 128 - HALO, main, edge)
            left_out[ch] = jnp.where(lane < HALO, main, edge)


def middle(scal, dual, before, pair):
    side = jax.ShapeDtypeStruct((8, 40, 128), F32)
    field = sent_out(8, 80, 128)
    return pl.pallas_call(
        middle_kernel,
        grid=(3,),
        in_specs=[SMEM, whole(8, 32, 128), whole(8, 64, 128), THIRD],
        out_specs=[THIRD, whole(8, 80, 128)] + [whole(8, 40, 128)] * 2 + [whole(8, 80, 128)],
        out_shape=[sent_out(NBASIS, 8, 32, 128), field, side, side, field],
        scratch_shapes=[FIELD, TURNED, PADDED, TURNED],
        compiler_params=params(20),
        cost_estimate=cost(6),
        name="middle",
    )(scal, in_hbm(before), in_hbm(pair), in_hbm(dual))


def last_kernel(scal_ref, now_ref, part_ref, above_ref, below_ref, gradient_ref, dual_ref,
                image_out, dual_out, field_ref, turned_ref):
    step_index = pl.program_id(0)

    @pl.when(step_index == 0)
    def first():
        chip_row, facet = where_am_i()[2:]
        lane = lanes_of((40, 128))
        row = lax.broadcasted_iota(jnp.int32, (40, 128), 0) + (32 * chip_row - HALO)
        in_rows = (row >= 0) & (row < 512)
        in_edge = ((lane < HALO) & (facet < 7)) | ((lane >= 128 - HALO) & (facet > 0))
        for ch in range(8):
            for start, keep in ((0, in_rows), (40, in_rows & in_edge)):
                which = start // 40
                gradient = unpacked_edge(gradient_ref[ch, 40:]) if which else gradient_ref[ch, :40]
                field_ref[ch, start : start + 40] = part_ref[ch, start : start + 40] + gradient
                field_ref[ch, start : start + 8] += above_ref[ch, which]
                field_ref[ch, start + 32 : start + 40] += below_ref[ch, which]
                now = now_ref[ch, start : start + 40]
                value = jnp.maximum(now - 0.5 * field_ref[ch, start : start + 40], 0.0)
                value = jnp.where(keep, value, 0.0)
                if start == 0:
                    image_out[ch] = value[HALO : HALO + 32]
                field_ref[ch, start : start + 40] = 2.0 * value - now
        shifted_columns(field_ref, turned_ref)

    @pl.loop(0, 3)
    def basis(i):
        shrink(scal_ref, 3 * step_index + i, i, dual_ref, turned_ref, dual_out)


def last(scal, dual, now, part, above, below, gradient):
    field, side = whole(8, 80, 128), whole(8, 2, 8, 128)
    return pl.pallas_call(
        last_kernel,
        grid=(3,),
        in_specs=[SMEM, field, field, side, side, whole(8, 48, 128), THIRD],
        out_specs=[whole(8, 32, 128), THIRD],
        out_shape=[
            jax.ShapeDtypeStruct((8, 32, 128), F32),
            jax.ShapeDtypeStruct((NBASIS, 8, 32, 128), F32),
        ],
        scratch_shapes=[FIELD, TURNED],
        compiler_params=params(20),
        cost_estimate=cost(4),
        name="last",
    )(scal, now, part, above, below, gradient, dual)


def swapped(value):
    return lax.ppermute(value, "core", [(0, 1), (1, 0)])


def neighbours(value, axis, count, step):
    return lax.ppermute(
        value, axis, [(i, i + step) for i in range(count) if 0 <= i + step < count]
    )


def half_of(value, half, size, dim):
    return lax.dynamic_slice_in_dim(value, half * size, size, dim)


def per_device(
    sky_image,
    dual_coefs,
    phase_screen,
    grid_rows,
    grid_weight,
    visibilities,
    filters,
    level_counts,
    radius,
):
    half, chip = where_am_i()[:2]
    scal = jnp.concatenate(
        [filters.reshape(NBASIS, 6), radius[:, None], level_counts[:, None].astype(F32)], axis=1
    )

    packed, phase = lax.optimization_barrier(
        (start(filters, level_counts, sky_image, dual_coefs), phase_screen[0, 0])
    )
    sent = lax.all_to_all(packed, "chan", 0, 0, tiled=True)

    phase_other = swapped(half_of(phase, 1 - half, 512, 1))
    weight_own = grid_weight[0, 0]
    weight_other = swapped(weight_own)
    data_own = visibilities[0, 0].reshape(128, 256)
    data = jnp.stack([data_own, swapped(data_own)])
    rows_own = grid_rows[0, 0]
    rows_other = swapped(rows_own.astype(F32)).astype(jnp.int32)
    left, right = tables(jnp.stack([rows_own, rows_other]))
    trig = screens(phase, phase_other)
    sent, left, right, trig = lax.optimization_barrier((sent, left, right, trig))

    own, other, term_own, term_other = split(sent)
    image = lax.all_to_all(spread(own, swapped(other)), CHIPS, 0, 0, tiled=True)
    extra = join(term_own, swapped(term_other))
    grid = gridding(weight_own, weight_other)
    image, extra, data = lax.optimization_barrier((image, extra, data))
    image = image.reshape(512, 512)

    seen, seen_copy = forward(image, trig, left, grid)
    window = lax.dynamic_slice_in_dim(jnp.pad(image, ((HALO, HALO), (0, 0))), 64 * chip, 72, 0)
    sent = backward(seen_copy, swapped(seen), data, grid, right, trig, extra)
    sent = lax.all_to_all(sent, CHIPS, 0, 0, tiled=True)
    own, other, many = update(sent, window)

    image = lax.all_to_all(many, CHIPS, 0, 0, tiled=True)
    packed = pair_to_facets(own, other)
    image, packed = lax.optimization_barrier((image, packed))
    image = image.reshape(512, 512)
    pair = lax.all_to_all(packed, "chan", 0, 0, tiled=True)
    seen, seen_copy = forward(image, trig, left, grid)
    dual, part, to_right, to_left, now = middle(scal, dual_coefs, sky_image, pair)
    sent = backward(seen_copy, swapped(seen), data, grid, right, trig)
    sent = lax.all_to_all(sent, CHIPS, 0, 0, tiled=True)
    from_left = neighbours(to_right, "chan", 8, 1)
    from_right = neighbours(to_left, "chan", 8, -1)
    packed = to_facets(*total_windows(sent))
    from_left, from_right = lax.optimization_barrier((from_left, from_right, packed))[:2]
    lane = lanes_of((8, 40, 128))
    main = part[:, :40] + jnp.where(lane < HALO, from_left, 0.0)
    main = main + jnp.where(lane >= 128 - HALO, from_right, 0.0)
    edge = part[:, 40:] + jnp.where(lane >= 128 - HALO, from_left, 0.0)
    edge = edge + jnp.where(lane < HALO, from_right, 0.0)
    both = jnp.stack([main, edge], axis=1)
    above = neighbours(both[:, :, 32:], ("y", "x", "core"), 16, 1)
    below = neighbours(both[:, :, :8], ("y", "x", "core"), 16, -1)
    gradient = lax.all_to_all(packed, "chan", 0, 0, tiled=True)
    return tuple(last(scal, dual, now, both.reshape(8, 80, 128), above, below, gradient))


def solution(mesh):
    fine = Mesh(mesh.devices.reshape(8, 2, 4, 2), ("chan", "y", "x", "core"))
    rows = ("y", "x", "core")
    placed = (
        P(None, rows, "chan"),
        P(None, None, rows, "chan"),
        P("chan", rows, None, None),
        P("chan", rows, None),
        P("chan", rows, None, None),
        P("chan", rows, None, None, None),
        P(),
        P(),
        P(),
    )
    return jax.shard_map(
        per_device,
        mesh=fine,
        in_specs=placed,
        out_specs=(P(None, rows, "chan"), P(None, None, rows, "chan")),
        check_vma=False,
    )
```

```python
import functools
import math

import jax
import jax.numpy as jnp
import ml_dtypes
import numpy as np
from jax import lax
from jax.experimental import pallas as pl
from jax.experimental.pallas import tpu as pltpu
from jax.sharding import Mesh
from jax.sharding import PartitionSpec as P

NBASIS = 9
HALO = 4
CHIPS = ("y", "x")
F32 = jnp.float32
BF16 = jnp.bfloat16
STEPS = (1, 2, 4)
SHIFTS = (0, -1, 1, -2, 2, -4, 4)
MIB = 1024 * 1024
SMEM = pl.BlockSpec(memory_space=pltpu.SMEM)
VMEM = pl.BlockSpec(memory_space=pltpu.VMEM)
ANY = pl.BlockSpec(memory_space=pltpu.HBM)


def params(size=16):
    return pltpu.CompilerParams(vmem_limit_bytes=size * MIB)


def where_am_i():
    half = lax.axis_index("core")
    chip = lax.axis_index("y") * 4 + lax.axis_index("x")
    return half, chip, 2 * chip + half, lax.axis_index("chan")


def cost(us):
    return pl.CostEstimate(flops=0, bytes_accessed=int(us * 3.0e6), transcendentals=0)


def sent_out(*shape):
    return pltpu.HBM(shape, F32)


def kept(shape, kind=F32):
    return pltpu.VMEM(shape, kind)


def in_hbm(value):
    return pltpu.with_memory_space_constraint(value, pltpu.HBM)


def chip_of(other_y, ahead):
    y = lax.axis_index("y")
    return 4 * ((1 - y) if other_y else y) + ((lax.axis_index("x") + ahead) & 3)


def parts(value):
    high = value.astype(BF16)
    return high, (value - high.astype(F32)).astype(BF16)


def dot(left, right):
    return jnp.dot(left, right, preferred_element_type=F32)


def dot_t(left, right):
    return lax.dot_general(left, right, (((1,), (1,)), ((), ())), preferred_element_type=F32)


def sincos(angle):
    y = 0.5 * angle
    z = y * y
    s = F32(2.6050929582509915e-06)
    for a in (-0.00019809011067269285, 0.008333050086782038, -0.16666657944392363, 0.9999999956966753):
        s = s * z + F32(a)
    s = s * y
    c = F32(-2.6050510628158867e-07)
    for a in (
        2.476010151557824e-05,
        -0.0013888360127752544,
        0.041666636147634536,
        -0.4999999935511792,
        0.9999999997790222,
    ):
        c = c * z + F32(a)
    return 2.0 * s * c, 1.0 - 2.0 * s * s


def rounded(value):
    return ((value * 32767.0 + 32768.5).astype(jnp.int32) - 32768).astype(jnp.int16)


def widened(value):
    return value.astype(jnp.int32).astype(F32)


def screens_kernel(other_ref, phase_hbm, out_ref, own_ref, sems):
    cols = pl.ds(pl.multiple_of(512 * lax.axis_index("core"), 512), 512)
    copies = [
        pltpu.make_async_copy(
            phase_hbm.at[pl.ds(128 * i, 128), cols], own_ref.at[pl.ds(128 * i, 128)], sems.at[i]
        )
        for i in range(4)
    ]
    for copy in copies:
        copy.start()

    def fill(b, ref, start):
        at = pl.ds(pl.multiple_of(start, 32), 32)
        s, c = sincos(ref[at])
        for part in range(2):
            cols = slice(256 * part, 256 * part + 256)
            out_ref[b, part, 0, at] = rounded(c[:, cols])
            out_ref[b, part, 1, at] = rounded(s[:, cols])

    pl.loop(0, 512, step=32)(functools.partial(fill, 1, other_ref))
    for i in range(4):
        copies[i].wait()
        pl.loop(128 * i, 128 * i + 128, step=32)(functools.partial(fill, 0, own_ref))


def screens(phase, other):
    return pl.pallas_call(
        screens_kernel,
        in_specs=[VMEM, ANY],
        out_specs=VMEM,
        out_shape=kept((2, 2, 2, 512, 256), jnp.int16),
        scratch_shapes=[pltpu.VMEM((512, 512), F32), pltpu.SemaphoreType.DMA((4,))],
        compiler_params=params(),
        cost_estimate=cost(4),
        name="screens",
    )(other, in_hbm(phase))


def tables_kernel(gcol_ref, grow_ref, left_ref, right_ref):
    size = 512
    for b in range(2):
        for turned, g_ref, out_ref in ((0, gcol_ref, left_ref), (1, grow_ref, right_ref)):
            shape = (size, 128) if turned else (128, size)
            n = lax.broadcasted_iota(jnp.int32, shape, 0 if turned else 1)
            picked = lax.broadcasted_iota(jnp.int32, shape, 1 if turned else 0)
            index = (g_ref[b] * n) & (size - 1)
            index = jnp.where(index >= size // 2, index - size, index)
            s, c = sincos(index.astype(F32) * F32(2.0 * math.pi / size))
            high, low = parts(jnp.where(picked < 64, c, -s) * F32(1.0 / math.sqrt(size)))
            if turned:
                out_ref[b, :, :128] = high
                out_ref[b, :, 128:] = low
            else:
                out_ref[b, :128, :] = high
                out_ref[b, 128:, :] = low


def tables(rows_both):
    doubled = jnp.concatenate([rows_both, rows_both], axis=1)
    return pl.pallas_call(
        tables_kernel,
        in_specs=[VMEM, VMEM],
        out_specs=[VMEM, VMEM],
        out_shape=[
            pltpu.HBM((2, 256, 512), BF16),
            pltpu.HBM((2, 512, 256), BF16),
        ],
        compiler_params=params(),
        cost_estimate=cost(2),
        name="tables",
    )(doubled[:, :, None], doubled[:, None, :])


def gridding_kernel(own_ref, other_ref, table_ref, out_ref):
    half = lax.axis_index("core")
    odd = lax.broadcasted_iota(jnp.int32, own_ref.shape, 0) & half
    sign = jnp.where(odd == 1, F32(-1.0), F32(1.0))
    for b, ref in enumerate((own_ref, other_ref)):
        high, low = parts(ref[...] * sign)
        for part in range(2):
            value = dot(table_ref[part, 0], high)
            value = value + dot(table_ref[part, 0], low)
            value = value + dot(table_ref[part, 1], high)
            for cols in range(2):
                kept_high, kept_low = parts(value[256 * cols : 256 * cols + 256])
                out_ref[b, cols, part, 0] = kept_high
                out_ref[b, cols, part, 1] = kept_low


def column_table():
    angle = (np.arange(512)[:, None] * np.arange(1024)[None, :] % 1024) * (2.0 * np.pi / 1024)
    out = np.zeros((2, 2, 512, 1024), ml_dtypes.bfloat16)
    for part, value in enumerate((np.cos(angle) / 32.0, -np.sin(angle) / 32.0)):
        high = value.astype(ml_dtypes.bfloat16)
        out[part, 0] = high
        out[part, 1] = (value - high.astype(np.float64)).astype(ml_dtypes.bfloat16)
    return out


def gridding(own, other):
    return pl.pallas_call(
        gridding_kernel,
        in_specs=[VMEM, VMEM, VMEM],
        out_specs=VMEM,
        out_shape=pltpu.HBM((2, 2, 2, 2, 256, 256), BF16),
        compiler_params=params(),
        cost_estimate=cost(7),
        name="gridding",
    )(own, other, column_table())


def thrice(left, high, low, form):
    count = left.shape[0] // 2
    both = form(left, high)
    return both[:count] + both[count:] + form(left[:count], low)


def fetch(table_hbm, grid_hbm, table_ref, grid_ref, sems, order):
    copies = {}
    for i, key in enumerate(order):
        source, target = (table_hbm, table_ref) if len(key) == 1 else (grid_hbm, grid_ref)
        copies[key] = pltpu.make_async_copy(source.at[key], target.at[key], sems.at[i])
        copies[key].start()
    return copies


FETCHED = [
    pltpu.VMEM((2, 2, 2, 2, 256, 256), BF16),
    pltpu.SemaphoreType.DMA((6,)),
]


def forward_kernel(*refs, windows):
    pieces, (trig_ref, left_hbm, grid_hbm, out_ref, copy_ref) = refs[: -9 - windows], refs[-9 - windows : -4 - windows]
    image_ref, left_ref, grid_ref, sems = refs[-4:]
    order = [(0,), (0, 0), (0, 1), (1,), (1, 0), (1, 1)]
    copies = fetch(left_hbm, grid_hbm, left_ref, grid_ref, sems, order)
    for i, ref in enumerate(pieces):
        start = pl.multiple_of(64 * chip_of(i // 4, i % 4) + 8, 8)
        image_ref[pl.ds(start, 64)] = ref[...]
    if windows:
        image_ref[0:8] = jnp.zeros((8, 512), F32)
        image_ref[520:528] = jnp.zeros((8, 512), F32)
        refs[-5][...] = image_ref[pl.ds(pl.multiple_of(64 * chip_of(0, 0), 64), 80)][4:76]
    for b in range(2):
        total = None
        copies[(b,)].wait()
        left = left_ref[b]
        for part in range(2):
            image = image_ref[8:520, 256 * part : 256 * part + 256] * F32(1.0 / 32767.0)
            from_real = thrice(left, *parts(widened(trig_ref[b, part, 0]) * image), dot)
            from_imag = thrice(left, *parts(widened(trig_ref[b, part, 1]) * image), dot)
            spectrum = jnp.concatenate(
                [from_real[:64] - from_imag[64:], from_imag[:64] + from_real[64:]], axis=0
            )
            spectrum = jnp.concatenate(parts(spectrum), axis=0)
            copies[(b, part)].wait()
            by_real = thrice(spectrum, grid_ref[b, part, 0, 0], grid_ref[b, part, 0, 1], dot)
            by_imag = thrice(spectrum, grid_ref[b, part, 1, 0], grid_ref[b, part, 1, 1], dot)
            seen = jnp.concatenate(
                [by_real[:64] - by_imag[64:], by_imag[:64] + by_real[64:]], axis=0
            )
            total = seen if total is None else total + seen
        out_ref[b] = total
        copy_ref[b] = total


def forward(pieces, trig, left, grid, windows):
    shapes = [jax.ShapeDtypeStruct((2, 128, 256), F32)] * 2
    if windows:
        shapes = shapes + [jax.ShapeDtypeStruct((72, 512), F32)]
    return pl.pallas_call(
        functools.partial(forward_kernel, windows=windows),
        in_specs=[VMEM] * (len(pieces) + 1) + [ANY] * 2,
        out_specs=[VMEM] * len(shapes),
        out_shape=shapes,
        scratch_shapes=[pltpu.VMEM((528, 512), F32), pltpu.VMEM((2, 256, 512), BF16)] + FETCHED,
        compiler_params=params(20),
        cost_estimate=cost(5),
        name="forward",
    )(*pieces, trig, in_hbm(left), in_hbm(grid))


def backward_kernel(mine_ref, theirs_ref, data_ref, trig_ref, *rest):
    extra_ref = rest[0] if len(rest) == 8 else None
    right_hbm, grid_hbm, out_ref = rest[-7:-4]
    total_ref, right_ref, grid_ref, sems = rest[-4:]
    order = [(0, 0), (0,), (1, 0), (1,), (0, 1), (1, 1)]
    copies = fetch(right_hbm, grid_hbm, right_ref, grid_ref, sems, order)
    total_ref[0:8] = jnp.zeros((8, 512), F32)
    total_ref[512:520] = jnp.zeros((8, 512), F32)
    misfits = [
        jnp.concatenate(parts(mine_ref[b] + theirs_ref[1 - b] - data_ref[b]), axis=0) for b in range(2)
    ]
    for half in range(2):
        cols = slice(256 * half, 256 * half + 256)
        total = None
        for b in range(2):
            copies[(b, half)].wait()
            by_real = thrice(misfits[b], grid_ref[b, half, 0, 0], grid_ref[b, half, 0, 1], dot_t)
            by_imag = thrice(misfits[b], grid_ref[b, half, 1, 0], grid_ref[b, half, 1, 1], dot_t)
            real = by_real[:64] + by_imag[64:]
            imag = by_real[64:] - by_imag[:64]
            spread = jnp.concatenate(
                [jnp.concatenate([real, imag], axis=1), jnp.concatenate([imag, -real], axis=1)],
                axis=0,
            )
            high, low = parts(spread * F32(1.0 / 32767.0))
            if half == 0:
                copies[(b,)].wait()
            right = right_ref[b]
            pulled = dot(right, jnp.concatenate([high, high], axis=0)) + dot(right[:, :128], low)
            part = widened(trig_ref[b, half, 0]) * pulled[:, :256]
            part = part + widened(trig_ref[b, half, 1]) * pulled[:, 256:]
            total = part if total is None else total + part
        total_ref[4:516, cols] = total
    if extra_ref is not None:
        rows = pl.ds(pl.multiple_of(64 * chip_of(0, 0), 64), 72)
        total_ref[rows] += extra_ref[...]
    for chip in range(8):
        out_ref[chip] = total_ref[64 * chip : 64 * chip + 72]


def backward(mine, theirs, data, grid, right, trig, extra=None):
    args = [mine, theirs, data, trig] + ([] if extra is None else [extra])
    return pl.pallas_call(
        backward_kernel,
        in_specs=[VMEM] * len(args) + [ANY] * 2,
        out_specs=VMEM,
        out_shape=sent_out(8, 72, 512),
        scratch_shapes=[pltpu.VMEM((520, 512), F32), pltpu.VMEM((2, 512, 256), BF16)] + FETCHED,
        compiler_params=params(20),
        cost_estimate=cost(5),
        name="backward",
    )(*args, in_hbm(right), in_hbm(grid))


def update_kernel(sent_ref, image_ref, own_ref, other_ref, core_ref, scratch_ref):
    half, chip = where_am_i()[:2]
    total = sent_ref[0]
    for source in range(1, 8):
        total = total + sent_ref[source]
    row = lax.broadcasted_iota(jnp.int32, total.shape, 0) + (64 * chip - HALO)
    value = jnp.maximum(image_ref[...] - 0.5 * total, 0.0)
    scratch_ref[...] = jnp.where((row >= 0) & (row < 512), value, 0.0)
    for window_ref, start in ((own_ref, 32 * half), (other_ref, 32 - 32 * half)):
        rows = pl.ds(pl.multiple_of(start, 32), 40)
        window_ref[0] = scratch_ref[rows]
        window_ref[1] = image_ref[rows]
    core_ref[...] = scratch_ref[HALO : HALO + 64]


def update(sent, image):
    window = jax.ShapeDtypeStruct((2, 40, 512), F32)
    return pl.pallas_call(
        update_kernel,
        in_specs=[VMEM] * 2,
        out_specs=[VMEM] * 3,
        out_shape=[window, window, jax.ShapeDtypeStruct((64, 512), F32)],
        scratch_shapes=[pltpu.VMEM((72, 512), F32)],
        compiler_params=params(),
        cost_estimate=cost(1),
        name="update",
    )(sent, image)


def total_kernel(sent_ref, own_ref, other_ref, scratch_ref):
    half = lax.axis_index("core")
    total = sent_ref[0]
    for source in range(1, 8):
        total = total + sent_ref[source]
    scratch_ref[...] = total
    own_ref[...] = scratch_ref[pl.ds(pl.multiple_of(32 * half, 32), 40)]
    other_ref[...] = scratch_ref[pl.ds(pl.multiple_of(32 - 32 * half, 32), 40)]


def total_windows(sent):
    window = jax.ShapeDtypeStruct((40, 512), F32)
    return pl.pallas_call(
        total_kernel,
        in_specs=[VMEM],
        out_specs=[VMEM] * 2,
        out_shape=[window, window],
        scratch_shapes=[pltpu.VMEM((72, 512), F32)],
        compiler_params=params(),
        cost_estimate=cost(1),
        name="total_windows",
    )(sent)


def lanes_of(shape):
    return lax.broadcasted_iota(jnp.int32, shape, len(shape) - 1)


def packed_edge(edge):
    lane = lanes_of((8, 128))
    out = jnp.zeros((8, 128), F32)
    for g in range(5):
        turned = pltpu.roll(edge[8 * g : 8 * g + 8], 8 * g + HALO, 1)
        out = jnp.where((lane >= 8 * g) & (lane < 8 * g + 8), turned, out)
    return out


def unpacked_edge(packed):
    lane = lanes_of((40, 128))
    turned = [pltpu.roll(packed, 128 - HALO - 8 * g, 1) for g in range(5)]
    inside = (lane < HALO) | (lane >= 128 - HALO)
    return jnp.where(inside, jnp.concatenate(turned, axis=0), 0.0)


def to_facets_kernel(own_ref, theirs_ref, out_ref, full_ref):
    half = lax.axis_index("core")
    full_ref[0] = jnp.zeros((40, 128), F32)
    full_ref[9] = jnp.zeros((40, 128), F32)
    for i in range(4):
        full_ref[1 + 4 * half + i] = own_ref[:, 128 * i : 128 * i + 128]
        full_ref[5 - 4 * half + i] = theirs_ref[:, 128 * i : 128 * i + 128]
    lane = lanes_of((40, 128))
    for facet in range(8):
        out_ref[facet, :40] = full_ref[facet + 1]
        out_ref[facet, 40:] = packed_edge(
            jnp.where(lane < HALO, full_ref[facet + 2], full_ref[facet])
        )


def to_facets(own, other):
    theirs = swapped(other)
    return pl.pallas_call(
        to_facets_kernel,
        in_specs=[VMEM, VMEM],
        out_specs=VMEM,
        out_shape=sent_out(8, 48, 128),
        scratch_shapes=[pltpu.VMEM((10, 40, 128), F32)],
        compiler_params=params(),
        cost_estimate=cost(1),
        name="to_facets",
    )(own, theirs)


def pair_kernel(own_ref, theirs_ref, out_ref, full_ref):
    half = lax.axis_index("core")
    for which in range(2):
        full_ref[which, 0] = jnp.zeros((40, 128), F32)
        full_ref[which, 9] = jnp.zeros((40, 128), F32)
        for i in range(4):
            full_ref[which, 1 + 4 * half + i] = own_ref[which, :, 128 * i : 128 * i + 128]
            full_ref[which, 5 - 4 * half + i] = theirs_ref[which, :, 128 * i : 128 * i + 128]
    lane = lanes_of((40, 128))
    row = lax.broadcasted_iota(jnp.int32, (8, 128), 0)
    for facet in range(8):
        out_ref[facet, :40] = full_ref[0, facet + 1]
        for which in range(2):
            out_ref[facet, 40 + 8 * which : 48 + 8 * which] = packed_edge(
                jnp.where(lane < HALO, full_ref[which, facet + 2], full_ref[which, facet])
            )
        out_ref[facet, 56:64] = jnp.where(
            row < HALO, full_ref[1, facet + 1, 0:8], full_ref[1, facet + 1, 32:40]
        )


def pair_to_facets(own, theirs):
    return pl.pallas_call(
        pair_kernel,
        in_specs=[VMEM, VMEM],
        out_specs=VMEM,
        out_shape=sent_out(8, 64, 128),
        scratch_shapes=[pltpu.VMEM((2, 10, 40, 128), F32)],
        compiler_params=params(),
        cost_estimate=cost(1),
        name="pair_to_facets",
    )(own, theirs)


def split_kernel(sent_ref, image_own, image_other, term_own, term_other, full_ref):
    half = lax.axis_index("core")
    lane = lanes_of((40, 128))
    edges = [unpacked_edge(sent_ref[facet, 72:80]) for facet in range(8)]
    for facet in range(8):
        value = sent_ref[facet, 32:72]
        if facet > 0:
            value = value + jnp.where(lane < HALO, edges[facet - 1], 0.0)
        if facet < 7:
            value = value + jnp.where(lane >= 128 - HALO, edges[facet + 1], 0.0)
        full_ref[facet] = value
    for i in range(4):
        cols = slice(128 * i, 128 * i + 128)
        image_own[:, cols] = sent_ref[4 * half + i, 0:32]
        image_other[:, cols] = sent_ref[4 - 4 * half + i, 0:32]
        term_own[:, cols] = full_ref[4 * half + i]
        term_other[:, cols] = full_ref[4 - 4 * half + i]


def split(sent):
    return pl.pallas_call(
        split_kernel,
        in_specs=[VMEM],
        out_specs=[VMEM] * 4,
        out_shape=[
            jax.ShapeDtypeStruct((32, 512), F32),
            sent_out(32, 512),
            sent_out(40, 512),
            sent_out(40, 512),
        ],
        scratch_shapes=[pltpu.VMEM((8, 40, 128), F32)],
        compiler_params=params(),
        cost_estimate=cost(1),
        name="split",
    )(sent)


def rows_kernel(own_ref, theirs_ref, out_ref):
    half = lax.axis_index("core")
    for ref, start in ((own_ref, 32 * half), (theirs_ref, 32 - 32 * half)):
        out_ref[pl.ds(pl.multiple_of(start, 32), 32)] = ref[...]


def join_rows(own, theirs):
    return pl.pallas_call(
        rows_kernel,
        in_specs=[VMEM, VMEM],
        out_specs=VMEM,
        out_shape=jax.ShapeDtypeStruct((64, 512), F32),
        compiler_params=params(),
        cost_estimate=cost(1),
        name="join_rows",
    )(own, theirs)


def join_kernel(own_ref, theirs_ref, out_ref):
    half = lax.axis_index("core")
    out_ref[...] = jnp.zeros((72, 512), F32)
    for ref, start in ((own_ref, 32 * half), (theirs_ref, 32 - 32 * half)):
        rows = pl.ds(pl.multiple_of(start, 32), 40)
        out_ref[rows] += ref[...]


def join(own, theirs):
    return pl.pallas_call(
        join_kernel,
        in_specs=[VMEM, VMEM],
        out_specs=VMEM,
        out_shape=jax.ShapeDtypeStruct((72, 512), F32),
        compiler_params=params(),
        cost_estimate=cost(1),
        name="join",
    )(in_hbm(own), theirs)


def spread_rows(scal_ref, q, step, ch, field, padded_ref, total_ref):
    padded_ref[ch, 8:40] = field
    low, mid, high = HALO + step, HALO, HALO - step
    value = (
        scal_ref[q, 0] * padded_ref[ch, low : low + 40]
        + scal_ref[q, 1] * padded_ref[ch, mid : mid + 40]
        + scal_ref[q, 2] * padded_ref[ch, high : high + 40]
    )
    for e in range(3):
        total_ref[SHIFTS.index((e - 1) * step), ch] += scal_ref[q, 3 + e] * value


def clear(padded_ref, total_ref):
    for ch in range(8):
        padded_ref[ch, 0:8] = jnp.zeros((8, 128), F32)
        padded_ref[ch, 40:48] = jnp.zeros((8, 128), F32)
        for d in range(7):
            total_ref[d, ch] = jnp.zeros((40, 128), F32)


def shift_all(total_ref, ch):
    lane = lanes_of((40, 128))
    main = total_ref[0, ch]
    edge = jnp.zeros((40, 128), F32)
    for d, col in enumerate(SHIFTS):
        if col:
            turned = pltpu.roll(total_ref[d, ch], col % 128, 1)
            inside = (lane >= col) if col > 0 else (lane < 128 + col)
            main = main + jnp.where(inside, turned, 0.0)
            edge = edge + jnp.where(inside, 0.0, turned)
    return main, edge


def shifted_columns(field_ref, turned_ref):
    lane = lanes_of((40, 128))

    @pl.loop(0, 8)
    def channel(ch):
        main = field_ref[ch, :40]
        edge = field_ref[ch, 40:]
        for d, col in enumerate(SHIFTS):
            if col:
                inside = (lane < 128 - col) if col > 0 else (lane >= -col)
                turned_ref[d, ch] = jnp.where(
                    inside, pltpu.roll(main, -col % 128, 1), pltpu.roll(edge, -col % 128, 1)
                )
            else:
                turned_ref[d, ch] = main


def each_level(scal_ref, q, work):
    for level, step in enumerate(STEPS):
        pl.when(scal_ref[q, 7] == F32(level + 1))(functools.partial(work, step))


def shrink(scal_ref, q, at, dual_ref, turned_ref, out_ref, after=None):
    def at_level(step):
        low, mid, high = (SHIFTS.index(s) for s in (-step, 0, step))
        squares = jnp.zeros((32, 128), F32)
        for ch in range(8):
            across = (
                scal_ref[q, 3] * turned_ref[low, ch]
                + scal_ref[q, 4] * turned_ref[mid, ch]
                + scal_ref[q, 5] * turned_ref[high, ch]
            )
            value = (
                scal_ref[q, 0] * across[HALO - step : HALO - step + 32]
                + scal_ref[q, 1] * across[HALO : HALO + 32]
                + scal_ref[q, 2] * across[HALO + step : HALO + step + 32]
            )
            raised = dual_ref[at, ch] + 0.5 * value
            out_ref[at, ch] = raised
            squares = squares + raised * raised
        limit = scal_ref[q, 6]
        scale = limit / jnp.maximum(jnp.sqrt(squares), limit)
        for ch in range(8):
            value = out_ref[at, ch] * scale
            out_ref[at, ch] = value
            if after is not None:
                after(step, ch, value)

    each_level(scal_ref, q, at_level)


class Scalars:
    def __init__(self, filters_ref, level_ref):
        self.filters_ref = filters_ref
        self.level_ref = level_ref

    def __getitem__(self, at):
        q, column = at
        if column == 7:
            return self.level_ref[q].astype(F32)
        return self.filters_ref[column % 3, column // 3, q]


def start_kernel(filters_ref, level_ref, image_ref, dual_ref, out_ref, padded_ref, total_ref):
    step_index = pl.program_id(0)
    scal_ref = Scalars(filters_ref, level_ref)

    @pl.when(step_index == 0)
    def first():
        clear(padded_ref, total_ref)

    @pl.loop(0, 3)
    def basis(i):
        q = 3 * step_index + i

        def at_level(step):
            for ch in range(8):
                spread_rows(scal_ref, q, step, ch, dual_ref[i, ch], padded_ref, total_ref)

        each_level(scal_ref, q, at_level)

    @pl.when(step_index == 2)
    def final():
        for ch in range(8):
            main, edge = shift_all(total_ref, ch)
            out_ref[ch, 0:32] = image_ref[ch]
            out_ref[ch, 32:72] = main
            out_ref[ch, 72:80] = packed_edge(edge)


TURNED = pltpu.VMEM((7, 8, 40, 128), F32)
FIELD = pltpu.VMEM((8, 80, 128), F32)
PADDED = pltpu.VMEM((8, 48, 128), F32)
THIRD = pl.BlockSpec((3, 8, 32, 128), lambda i: (i, 0, 0, 0))


def whole(*shape):
    return pl.BlockSpec(shape, lambda i: (0,) * len(shape))


def start(filters, levels, image, dual):
    return pl.pallas_call(
        start_kernel,
        grid=(3,),
        in_specs=[SMEM, SMEM, whole(8, 32, 128), THIRD],
        out_specs=whole(8, 80, 128),
        out_shape=sent_out(8, 80, 128),
        scratch_shapes=[PADDED, TURNED],
        compiler_params=params(),
        cost_estimate=cost(4),
        name="start",
    )(filters, in_hbm(levels), in_hbm(image), in_hbm(dual))


def middle_kernel(scal_ref, before_ref, pair_ref, dual_ref, dual_out, part_out, right_out, left_out,
                  now_out, field_ref, turned_ref, padded_ref, total_ref):
    step_index = pl.program_id(0)

    @pl.when(step_index == 0)
    def first():
        for ch in range(8):
            main = pair_ref[ch, :40]
            now_out[ch, :40] = main
            now = 2.0 * main
            field_ref[ch, 4:36] = now[4:36] - before_ref[ch]
            outer = pair_ref[ch, 56:64]
            field_ref[ch, 0:4] = now[0:4] - outer[0:4]
            field_ref[ch, 36:40] = now[36:40] - outer[4:8]
            edge = unpacked_edge(pair_ref[ch, 40:48])
            now_out[ch, 40:] = edge
            field_ref[ch, 40:] = 2.0 * edge - unpacked_edge(pair_ref[ch, 48:56])
        shifted_columns(field_ref, turned_ref)
        clear(padded_ref, total_ref)

    @pl.loop(0, 3)
    def basis(i):
        q = 3 * step_index + i

        def after(step, ch, value):
            spread_rows(scal_ref, q, step, ch, value, padded_ref, total_ref)

        shrink(scal_ref, q, i, dual_ref, turned_ref, dual_out, after)

    @pl.when(step_index == 2)
    def final():
        lane = lanes_of((40, 128))
        for ch in range(8):
            main, edge = shift_all(total_ref, ch)
            part_out[ch, :40] = main
            part_out[ch, 40:] = edge
            right_out[ch] = jnp.where(lane >= 128 - HALO, main, edge)
            left_out[ch] = jnp.where(lane < HALO, main, edge)


def middle(scal, dual, before, pair):
    side = jax.ShapeDtypeStruct((8, 40, 128), F32)
    field = sent_out(8, 80, 128)
    return pl.pallas_call(
        middle_kernel,
        grid=(3,),
        in_specs=[SMEM, whole(8, 32, 128), whole(8, 64, 128), THIRD],
        out_specs=[THIRD, whole(8, 80, 128)] + [whole(8, 40, 128)] * 2 + [whole(8, 80, 128)],
        out_shape=[sent_out(NBASIS, 8, 32, 128), field, side, side, field],
        scratch_shapes=[FIELD, TURNED, PADDED, TURNED],
        compiler_params=params(20),
        cost_estimate=cost(7),
        name="middle",
    )(scal, in_hbm(before), pair, in_hbm(dual))


def last_kernel(scal_ref, now_ref, part_ref, above_ref, below_ref, gradient_ref, dual_ref,
                image_out, dual_out, field_ref, turned_ref):
    step_index = pl.program_id(0)

    @pl.when(step_index == 0)
    def first():
        chip_row, facet = where_am_i()[2:]
        lane = lanes_of((40, 128))
        row = lax.broadcasted_iota(jnp.int32, (40, 128), 0) + (32 * chip_row - HALO)
        in_rows = (row >= 0) & (row < 512)
        in_edge = ((lane < HALO) & (facet < 7)) | ((lane >= 128 - HALO) & (facet > 0))
        for ch in range(8):
            for start, keep in ((0, in_rows), (40, in_rows & in_edge)):
                which = start // 40
                gradient = unpacked_edge(gradient_ref[ch, 40:]) if which else gradient_ref[ch, :40]
                field_ref[ch, start : start + 40] = part_ref[ch, start : start + 40] + gradient
                field_ref[ch, start : start + 8] += above_ref[ch, which]
                field_ref[ch, start + 32 : start + 40] += below_ref[ch, which]
                now = now_ref[ch, start : start + 40]
                value = jnp.maximum(now - 0.5 * field_ref[ch, start : start + 40], 0.0)
                value = jnp.where(keep, value, 0.0)
                if start == 0:
                    image_out[ch] = value[HALO : HALO + 32]
                field_ref[ch, start : start + 40] = 2.0 * value - now
        shifted_columns(field_ref, turned_ref)

    @pl.loop(0, 3)
    def basis(i):
        shrink(scal_ref, 3 * step_index + i, i, dual_ref, turned_ref, dual_out)


def last(scal, dual, now, part, above, below, gradient):
    field, side = whole(8, 80, 128), whole(8, 2, 8, 128)
    return pl.pallas_call(
        last_kernel,
        grid=(3,),
        in_specs=[SMEM, field, field, side, side, whole(8, 48, 128), THIRD],
        out_specs=[whole(8, 32, 128), THIRD],
        out_shape=[
            jax.ShapeDtypeStruct((8, 32, 128), F32),
            jax.ShapeDtypeStruct((NBASIS, 8, 32, 128), F32),
        ],
        scratch_shapes=[FIELD, TURNED],
        compiler_params=params(20),
        cost_estimate=cost(4),
        name="last",
    )(scal, now, part, above, below, gradient, dual)


def swapped(value):
    return lax.ppermute(value, "core", [(0, 1), (1, 0)])


def gathered(value):
    return gathered_x(value) + gathered_x(across_y(value))


def across_y(value):
    return lax.ppermute(value, "y", [(0, 1), (1, 0)])


def along_x(value, step):
    return lax.ppermute(value, "x", [(i, (i + step) % 4) for i in range(4)])


def gathered_x(value):
    return [value] + [along_x(value, -ahead) for ahead in (1, 2, 3)]


def neighbours(value, axis, count, step):
    return lax.ppermute(
        value, axis, [(i, i + step) for i in range(count) if 0 <= i + step < count]
    )


def half_of(value, half, size, dim):
    return lax.dynamic_slice_in_dim(value, half * size, size, dim)


def per_device(
    sky_image,
    dual_coefs,
    phase_screen,
    grid_rows,
    grid_weight,
    visibilities,
    filters,
    level_counts,
    radius,
):
    half = lax.axis_index("core")
    scal = jnp.concatenate(
        [filters.reshape(NBASIS, 6), radius[:, None], level_counts[:, None].astype(F32)], axis=1
    )

    packed, phase = lax.optimization_barrier(
        (start(filters.transpose(2, 1, 0), level_counts, sky_image, dual_coefs), phase_screen[0, 0])
    )
    sent = lax.all_to_all(packed, "chan", 0, 0, tiled=True)

    phase_other = swapped(half_of(phase, 1 - half, 512, 1))
    weight_own = grid_weight[0, 0]
    weight_other = swapped(weight_own)
    data_own = visibilities[0, 0].reshape(128, 256)
    data = jnp.stack([data_own, swapped(data_own)])
    rows_own = grid_rows[0, 0]
    rows_other = swapped(rows_own.astype(F32)).astype(jnp.int32)
    left, right = tables(jnp.stack([rows_own, rows_other]))
    trig = screens(phase, phase_other)
    grid = gridding(weight_own, weight_other)
    sent, grid = lax.optimization_barrier((sent, grid))

    own, other, term_own, term_other = split(sent)
    strip = join_rows(own, swapped(other))
    pieces = gathered(strip)
    extra = join(term_own, swapped(term_other))
    pieces, extra, data, right = lax.optimization_barrier((pieces, extra, data, right))

    seen, seen_copy, window = forward(pieces, trig, left, grid, True)
    sent = backward(seen_copy, swapped(seen), data, grid, right, trig, extra)
    sent = lax.all_to_all(sent, CHIPS, 0, 0, tiled=True)
    own, other, core = update(sent, window)

    pieces = gathered(core)
    packed = pair_to_facets(own, swapped(other))
    packed, pieces[4] = lax.optimization_barrier((packed, pieces[4]))
    pair = lax.all_to_all(packed, "chan", 0, 0, tiled=True)
    seen, seen_copy = forward(pieces, trig, left, grid, False)
    dual, part, to_right, to_left, now = middle(scal, dual_coefs, sky_image, pair)
    sent = backward(seen_copy, swapped(seen), data, grid, right, trig)
    sent = lax.all_to_all(sent, CHIPS, 0, 0, tiled=True)
    windows = total_windows(sent)
    from_left = neighbours(to_right, "chan", 8, 1)
    from_right = neighbours(to_left, "chan", 8, -1)
    packed = to_facets(*windows)
    from_left, from_right = lax.optimization_barrier((from_left, from_right, packed))[:2]
    lane = lanes_of((8, 40, 128))
    main = part[:, :40] + jnp.where(lane < HALO, from_left, 0.0)
    main = main + jnp.where(lane >= 128 - HALO, from_right, 0.0)
    edge = part[:, 40:] + jnp.where(lane >= 128 - HALO, from_left, 0.0)
    edge = edge + jnp.where(lane < HALO, from_right, 0.0)
    both = jnp.stack([main, edge], axis=1)
    above = neighbours(both[:, :, 32:], ("y", "x", "core"), 16, 1)
    below = neighbours(both[:, :, :8], ("y", "x", "core"), 16, -1)
    gradient = lax.all_to_all(packed, "chan", 0, 0, tiled=True)
    return tuple(last(scal, dual, now, both.reshape(8, 80, 128), above, below, gradient))


def solution(mesh):
    fine = Mesh(mesh.devices.reshape(8, 2, 4, 2), ("chan", "y", "x", "core"))
    rows = ("y", "x", "core")
    placed = (
        P(None, rows, "chan"),
        P(None, None, rows, "chan"),
        P("chan", rows, None, None),
        P("chan", rows, None),
        P("chan", rows, None, None),
        P("chan", rows, None, None, None),
        P(),
        P(),
        P(),
    )
    return jax.shard_map(
        per_device,
        mesh=fine,
        in_specs=placed,
        out_specs=(P(None, rows, "chan"), P(None, None, rows, "chan")),
        check_vma=False,
    )
```

```python
import functools
import math

import jax
import jax.numpy as jnp
import ml_dtypes
import numpy as np
from jax import lax
from jax.experimental import pallas as pl
from jax.experimental.pallas import tpu as pltpu
from jax.sharding import Mesh
from jax.sharding import PartitionSpec as P

NBASIS = 9
HALO = 4
CHIPS = ("y", "x")
F32 = jnp.float32
BF16 = jnp.bfloat16
STEPS = (1, 2, 4)
SHIFTS = (0, -1, 1, -2, 2, -4, 4)
MIB = 1024 * 1024
SMEM = pl.BlockSpec(memory_space=pltpu.SMEM)
VMEM = pl.BlockSpec(memory_space=pltpu.VMEM)
ANY = pl.BlockSpec(memory_space=pltpu.HBM)


def params(size=16):
    return pltpu.CompilerParams(vmem_limit_bytes=size * MIB)


def where_am_i():
    half = lax.axis_index("core")
    chip = lax.axis_index("y") * 4 + lax.axis_index("x")
    return half, chip, 2 * chip + half, lax.axis_index("chan")


def cost(us):
    return pl.CostEstimate(flops=0, bytes_accessed=int(us * 3.0e6), transcendentals=0)


def sent_out(*shape):
    return pltpu.HBM(shape, F32)


def kept(shape, kind=F32):
    return pltpu.VMEM(shape, kind)


def in_hbm(value):
    return pltpu.with_memory_space_constraint(value, pltpu.HBM)


def chip_of(other_y, ahead):
    y = lax.axis_index("y")
    return 4 * ((1 - y) if other_y else y) + ((lax.axis_index("x") + ahead) & 3)


def parts(value):
    high = value.astype(BF16)
    return high, (value - high.astype(F32)).astype(BF16)


def dot(left, right):
    return jnp.dot(left, right, preferred_element_type=F32)


def dot_t(left, right):
    return lax.dot_general(left, right, (((1,), (1,)), ((), ())), preferred_element_type=F32)


def sincos(angle):
    y = 0.5 * angle
    z = y * y
    s = F32(2.6050929582509915e-06)
    for a in (-0.00019809011067269285, 0.008333050086782038, -0.16666657944392363, 0.9999999956966753):
        s = s * z + F32(a)
    s = s * y
    c = F32(-2.6050510628158867e-07)
    for a in (
        2.476010151557824e-05,
        -0.0013888360127752544,
        0.041666636147634536,
        -0.4999999935511792,
        0.9999999997790222,
    ):
        c = c * z + F32(a)
    return 2.0 * s * c, 1.0 - 2.0 * s * s


def rounded(value):
    return ((value * 32767.0 + 32768.5).astype(jnp.int32) - 32768).astype(jnp.int16)


def widened(value):
    return value.astype(jnp.int32).astype(F32)


def screens_kernel(other_ref, phase_hbm, out_ref, own_ref, sems):
    cols = pl.ds(pl.multiple_of(512 * lax.axis_index("core"), 512), 512)
    copies = [
        pltpu.make_async_copy(
            phase_hbm.at[pl.ds(128 * i, 128), cols], own_ref.at[pl.ds(128 * i, 128)], sems.at[i]
        )
        for i in range(4)
    ]
    for copy in copies:
        copy.start()

    def fill(b, ref, start):
        at = pl.ds(pl.multiple_of(start, 32), 32)
        s, c = sincos(ref[at])
        for part in range(2):
            cols = slice(256 * part, 256 * part + 256)
            out_ref[b, part, 0, at] = rounded(c[:, cols])
            out_ref[b, part, 1, at] = rounded(s[:, cols])

    pl.loop(0, 512, step=32)(functools.partial(fill, 1, other_ref))
    for i in range(4):
        copies[i].wait()
        pl.loop(128 * i, 128 * i + 128, step=32)(functools.partial(fill, 0, own_ref))


def screens(phase, other):
    return pl.pallas_call(
        screens_kernel,
        in_specs=[VMEM, ANY],
        out_specs=VMEM,
        out_shape=kept((2, 2, 2, 512, 256), jnp.int16),
        scratch_shapes=[pltpu.VMEM((512, 512), F32), pltpu.SemaphoreType.DMA((4,))],
        compiler_params=params(),
        cost_estimate=cost(4),
        name="screens",
    )(other, in_hbm(phase))


def tables_kernel(gcol_ref, grow_ref, left_ref, right_ref):
    size = 512
    for b in range(2):
        for turned, g_ref, out_ref in ((0, gcol_ref, left_ref), (1, grow_ref, right_ref)):
            shape = (size, 128) if turned else (128, size)
            n = lax.broadcasted_iota(jnp.int32, shape, 0 if turned else 1)
            picked = lax.broadcasted_iota(jnp.int32, shape, 1 if turned else 0)
            index = (g_ref[b] * n) & (size - 1)
            index = jnp.where(index >= size // 2, index - size, index)
            s, c = sincos(index.astype(F32) * F32(2.0 * math.pi / size))
            high, low = parts(jnp.where(picked < 64, c, -s) * F32(1.0 / math.sqrt(size)))
            if turned:
                out_ref[b, :, :128] = high
                out_ref[b, :, 128:] = low
            else:
                out_ref[b, :128, :] = high
                out_ref[b, 128:, :] = low


def tables(rows_both):
    doubled = jnp.concatenate([rows_both, rows_both], axis=1)
    return pl.pallas_call(
        tables_kernel,
        in_specs=[VMEM, VMEM],
        out_specs=[VMEM, VMEM],
        out_shape=[
            pltpu.HBM((2, 256, 512), BF16),
            pltpu.HBM((2, 512, 256), BF16),
        ],
        compiler_params=params(),
        cost_estimate=cost(2),
        name="tables",
    )(doubled[:, :, None], doubled[:, None, :])


def gridding_kernel(own_ref, other_ref, table_ref, turn_ref, out_ref, first_ref, second_ref):
    half = lax.axis_index("core")
    sign = jnp.where(half == 1, F32(-1.0), F32(1.0))
    table = table_ref[...]
    for b, ref in enumerate((own_ref, other_ref)):
        turned = []
        first_ref[...] = ref[:, :128]
        second_ref[...] = ref[:, 128:]
        for q in range(4):
            rows = pl.ds(q, 256, stride=4)
            high, low = parts(jnp.concatenate([first_ref[rows], second_ref[rows]], axis=1))
            value = dot(table, high)
            real = value[0:256] + value[256:512]
            imag = value[512:768] + value[768:1024]
            value = dot(table[0:256], low)
            real = real + value
            value = dot(table[512:768], low)
            imag = imag + value
            if q:
                cos, sin = turn_ref[:, 2 * q : 2 * q + 1], turn_ref[:, 2 * q + 1 : 2 * q + 2]
                if q & 1:
                    cos, sin = cos * sign, sin * sign
                real, imag = cos * real + sin * imag, cos * imag - sin * real
            turned.append((real, imag))
        even = [turned[0][i] + turned[2][i] for i in range(2)]
        odd = [turned[1][i] + turned[3][i] for i in range(2)]
        near = [even[i] + odd[i] for i in range(2)]
        even = [turned[0][i] - turned[2][i] for i in range(2)]
        odd = [turned[1][i] - turned[3][i] for i in range(2)]
        far = [even[0] + odd[1], even[1] - odd[0]]
        for cols, values in enumerate((near, far)):
            for part in range(2):
                high, low = parts(values[part])
                out_ref[b, cols, part, 0] = high
                out_ref[b, cols, part, 1] = low


def column_table():
    angle = (np.arange(256)[:, None] * np.arange(256)[None, :] % 256) * (2.0 * np.pi / 256)
    out = np.zeros((4, 256, 256), ml_dtypes.bfloat16)
    for part, value in enumerate((np.cos(angle) / 32.0, -np.sin(angle) / 32.0)):
        high = value.astype(ml_dtypes.bfloat16)
        out[2 * part] = high
        out[2 * part + 1] = (value - high.astype(np.float64)).astype(ml_dtypes.bfloat16)
    return out.reshape(1024, 256)


def turns():
    out = np.zeros((256, 8), np.float32)
    for q in range(4):
        angle = np.arange(256) * q * (2.0 * np.pi / 1024)
        out[:, 2 * q] = np.cos(angle)
        out[:, 2 * q + 1] = np.sin(angle)
    return out


def gridding(own, other):
    return pl.pallas_call(
        gridding_kernel,
        in_specs=[VMEM] * 4,
        out_specs=VMEM,
        out_shape=pltpu.HBM((2, 2, 2, 2, 256, 256), BF16),
        scratch_shapes=[pltpu.VMEM((1024, 128), F32)] * 2,
        compiler_params=params(),
        cost_estimate=cost(3),
        name="gridding",
    )(own, other, column_table(), turns())


def thrice(left, high, low, form):
    count = left.shape[0] // 2
    both = form(left, high)
    return both[:count] + both[count:] + form(left[:count], low)


def fetch(table_hbm, grid_hbm, table_ref, grid_ref, sems, order):
    copies = {}
    for i, key in enumerate(order):
        source, target = (table_hbm, table_ref) if len(key) == 1 else (grid_hbm, grid_ref)
        copies[key] = pltpu.make_async_copy(source.at[key], target.at[key], sems.at[i])
        copies[key].start()
    return copies


FETCHED = [
    pltpu.VMEM((2, 2, 2, 2, 256, 256), BF16),
    pltpu.SemaphoreType.DMA((6,)),
]


def forward_kernel(*refs, windows):
    pieces, (trig_ref, left_hbm, grid_hbm, out_ref, copy_ref) = refs[: -9 - windows], refs[-9 - windows : -4 - windows]
    image_ref, left_ref, grid_ref, sems = refs[-4:]
    order = [(0,), (0, 0), (0, 1), (1,), (1, 0), (1, 1)]
    copies = fetch(left_hbm, grid_hbm, left_ref, grid_ref, sems, order)
    for i, ref in enumerate(pieces):
        start = pl.multiple_of(64 * chip_of(i // 4, i % 4) + 8, 8)
        image_ref[pl.ds(start, 64)] = ref[...]
    if windows:
        image_ref[0:8] = jnp.zeros((8, 512), F32)
        image_ref[520:528] = jnp.zeros((8, 512), F32)
        refs[-5][...] = image_ref[pl.ds(pl.multiple_of(64 * chip_of(0, 0), 64), 80)][4:76]
    for b in range(2):
        total = None
        copies[(b,)].wait()
        left = left_ref[b]
        for part in range(2):
            image = image_ref[8:520, 256 * part : 256 * part + 256] * F32(1.0 / 32767.0)
            from_real = thrice(left, *parts(widened(trig_ref[b, part, 0]) * image), dot)
            from_imag = thrice(left, *parts(widened(trig_ref[b, part, 1]) * image), dot)
            spectrum = jnp.concatenate(
                [from_real[:64] - from_imag[64:], from_imag[:64] + from_real[64:]], axis=0
            )
            spectrum = jnp.concatenate(parts(spectrum), axis=0)
            copies[(b, part)].wait()
            by_real = thrice(spectrum, grid_ref[b, part, 0, 0], grid_ref[b, part, 0, 1], dot)
            by_imag = thrice(spectrum, grid_ref[b, part, 1, 0], grid_ref[b, part, 1, 1], dot)
            seen = jnp.concatenate(
                [by_real[:64] - by_imag[64:], by_imag[:64] + by_real[64:]], axis=0
            )
            total = seen if total is None else total + seen
        out_ref[b] = total
        copy_ref[b] = total


def forward(pieces, trig, left, grid, windows):
    shapes = [jax.ShapeDtypeStruct((2, 128, 256), F32)] * 2
    if windows:
        shapes = shapes + [jax.ShapeDtypeStruct((72, 512), F32)]
    return pl.pallas_call(
        functools.partial(forward_kernel, windows=windows),
        in_specs=[VMEM] * (len(pieces) + 1) + [ANY] * 2,
        out_specs=[VMEM] * len(shapes),
        out_shape=shapes,
        scratch_shapes=[pltpu.VMEM((528, 512), F32), pltpu.VMEM((2, 256, 512), BF16)] + FETCHED,
        compiler_params=params(20),
        cost_estimate=cost(5),
        name="forward",
    )(*pieces, trig, in_hbm(left), in_hbm(grid))


def backward_kernel(mine_ref, theirs_ref, data_ref, trig_ref, *rest):
    extra_ref = rest[0] if len(rest) == 15 else None
    right_hbm, grid_hbm, *outs = rest[-7:-4] if extra_ref is None else rest[-14:-4]
    total_ref, right_ref, grid_ref, sems = rest[-4:]
    order = [(0, 0), (0,), (1, 0), (1,), (0, 1), (1, 1)]
    copies = fetch(right_hbm, grid_hbm, right_ref, grid_ref, sems, order)
    total_ref[0:8] = jnp.zeros((8, 512), F32)
    total_ref[512:520] = jnp.zeros((8, 512), F32)
    misfits = [
        jnp.concatenate(parts(mine_ref[b] + theirs_ref[1 - b] - data_ref[b]), axis=0) for b in range(2)
    ]
    for half in range(2):
        cols = slice(256 * half, 256 * half + 256)
        total = None
        for b in range(2):
            copies[(b, half)].wait()
            by_real = thrice(misfits[b], grid_ref[b, half, 0, 0], grid_ref[b, half, 0, 1], dot_t)
            by_imag = thrice(misfits[b], grid_ref[b, half, 1, 0], grid_ref[b, half, 1, 1], dot_t)
            real = by_real[:64] + by_imag[64:]
            imag = by_real[64:] - by_imag[:64]
            spread = jnp.concatenate(
                [jnp.concatenate([real, imag], axis=1), jnp.concatenate([imag, -real], axis=1)],
                axis=0,
            )
            high, low = parts(spread * F32(1.0 / 32767.0))
            if half == 0:
                copies[(b,)].wait()
            right = right_ref[b]
            pulled = dot(right, jnp.concatenate([high, high], axis=0)) + dot(right[:, :128], low)
            part = widened(trig_ref[b, half, 0]) * pulled[:, :256]
            part = part + widened(trig_ref[b, half, 1]) * pulled[:, 256:]
            total = part if total is None else total + part
        total_ref[4:516, cols] = total
    if extra_ref is not None:
        rows = pl.ds(pl.multiple_of(64 * chip_of(0, 0), 64), 72)
        total_ref[rows] += extra_ref[...]
    if extra_ref is None:
        for chip in range(8):
            outs[0][chip] = total_ref[64 * chip : 64 * chip + 72]
    else:
        for i, ref in enumerate(outs):
            ref[...] = total_ref[pl.ds(pl.multiple_of(64 * chip_of(i // 4, i % 4), 64), 72)]


def backward(mine, theirs, data, grid, right, trig, extra=None):
    args = [mine, theirs, data, trig] + ([] if extra is None else [extra])
    pieces = [jax.ShapeDtypeStruct((72, 512), F32)] * 8
    return pl.pallas_call(
        backward_kernel,
        in_specs=[VMEM] * len(args) + [ANY] * 2,
        out_specs=VMEM if extra is None else [VMEM] * 8,
        out_shape=sent_out(8, 72, 512) if extra is None else pieces,
        scratch_shapes=[pltpu.VMEM((520, 512), F32), pltpu.VMEM((2, 512, 256), BF16)] + FETCHED,
        compiler_params=params(20),
        cost_estimate=cost(5),
        name="backward",
    )(*args, in_hbm(right), in_hbm(grid))


def sum_of(refs):
    total = refs[0][...]
    for ref in refs[1:]:
        total = total + ref[...]
    return total


def update_kernel(*refs):
    image_ref, own_ref, other_ref, core_ref, scratch_ref = refs[8:]
    half, chip = where_am_i()[:2]
    total = sum_of(refs[:8])
    row = lax.broadcasted_iota(jnp.int32, total.shape, 0) + (64 * chip - HALO)
    value = jnp.maximum(image_ref[...] - 0.5 * total, 0.0)
    scratch_ref[...] = jnp.where((row >= 0) & (row < 512), value, 0.0)
    for window_ref, start in ((own_ref, 32 * half), (other_ref, 32 - 32 * half)):
        rows = pl.ds(pl.multiple_of(start, 32), 40)
        window_ref[0] = scratch_ref[rows]
        window_ref[1] = image_ref[rows]
    core_ref[...] = scratch_ref[HALO : HALO + 64]


def update(sent, image):
    window = jax.ShapeDtypeStruct((2, 40, 512), F32)
    return pl.pallas_call(
        update_kernel,
        in_specs=[VMEM] * 9,
        out_specs=[VMEM] * 3,
        out_shape=[window, window, jax.ShapeDtypeStruct((64, 512), F32)],
        scratch_shapes=[pltpu.VMEM((72, 512), F32)],
        compiler_params=params(),
        cost_estimate=cost(1),
        name="update",
    )(*sent, image)


def total_kernel(sent_ref, own_ref, other_ref, scratch_ref):
    half = lax.axis_index("core")
    scratch_ref[...] = sum_of([sent_ref.at[source] for source in range(8)])
    own_ref[...] = scratch_ref[pl.ds(pl.multiple_of(32 * half, 32), 40)]
    other_ref[...] = scratch_ref[pl.ds(pl.multiple_of(32 - 32 * half, 32), 40)]


def total_windows(sent):
    window = jax.ShapeDtypeStruct((40, 512), F32)
    return pl.pallas_call(
        total_kernel,
        in_specs=[VMEM],
        out_specs=[VMEM] * 2,
        out_shape=[window, window],
        scratch_shapes=[pltpu.VMEM((72, 512), F32)],
        compiler_params=params(),
        cost_estimate=cost(1),
        name="total_windows",
    )(sent)


def lanes_of(shape):
    return lax.broadcasted_iota(jnp.int32, shape, len(shape) - 1)


def packed_edge(edge):
    lane = lanes_of((8, 128))
    out = jnp.zeros((8, 128), F32)
    for g in range(5):
        turned = pltpu.roll(edge[8 * g : 8 * g + 8], 8 * g + HALO, 1)
        out = jnp.where((lane >= 8 * g) & (lane < 8 * g + 8), turned, out)
    return out


def unpacked_edge(packed):
    lane = lanes_of((40, 128))
    turned = [pltpu.roll(packed, 128 - HALO - 8 * g, 1) for g in range(5)]
    inside = (lane < HALO) | (lane >= 128 - HALO)
    return jnp.where(inside, jnp.concatenate(turned, axis=0), 0.0)


def to_facets_kernel(own_ref, theirs_ref, out_ref, full_ref):
    half = lax.axis_index("core")
    full_ref[0] = jnp.zeros((40, 128), F32)
    full_ref[9] = jnp.zeros((40, 128), F32)
    for i in range(4):
        full_ref[1 + 4 * half + i] = own_ref[:, 128 * i : 128 * i + 128]
        full_ref[5 - 4 * half + i] = theirs_ref[:, 128 * i : 128 * i + 128]
    lane = lanes_of((40, 128))
    for facet in range(8):
        out_ref[facet, :40] = full_ref[facet + 1]
        out_ref[facet, 40:] = packed_edge(
            jnp.where(lane < HALO, full_ref[facet + 2], full_ref[facet])
        )


def to_facets(own, other):
    theirs = swapped(other)
    return pl.pallas_call(
        to_facets_kernel,
        in_specs=[VMEM, VMEM],
        out_specs=VMEM,
        out_shape=sent_out(8, 48, 128),
        scratch_shapes=[pltpu.VMEM((10, 40, 128), F32)],
        compiler_params=params(),
        cost_estimate=cost(1),
        name="to_facets",
    )(own, theirs)


def pair_kernel(own_ref, theirs_ref, out_ref, full_ref):
    half = lax.axis_index("core")
    for which in range(2):
        full_ref[which, 0] = jnp.zeros((40, 128), F32)
        full_ref[which, 9] = jnp.zeros((40, 128), F32)
        for i in range(4):
            full_ref[which, 1 + 4 * half + i] = own_ref[which, :, 128 * i : 128 * i + 128]
            full_ref[which, 5 - 4 * half + i] = theirs_ref[which, :, 128 * i : 128 * i + 128]
    lane = lanes_of((40, 128))
    row = lax.broadcasted_iota(jnp.int32, (8, 128), 0)
    for facet in range(8):
        out_ref[facet, :40] = full_ref[0, facet + 1]
        for which in range(2):
            out_ref[facet, 40 + 8 * which : 48 + 8 * which] = packed_edge(
                jnp.where(lane < HALO, full_ref[which, facet + 2], full_ref[which, facet])
            )
        out_ref[facet, 56:64] = jnp.where(
            row < HALO, full_ref[1, facet + 1, 0:8], full_ref[1, facet + 1, 32:40]
        )


def pair_to_facets(own, theirs):
    return pl.pallas_call(
        pair_kernel,
        in_specs=[VMEM, VMEM],
        out_specs=VMEM,
        out_shape=sent_out(8, 64, 128),
        scratch_shapes=[pltpu.VMEM((2, 10, 40, 128), F32)],
        compiler_params=params(),
        cost_estimate=cost(1),
        name="pair_to_facets",
    )(own, theirs)


def split_kernel(sent_ref, image_own, image_other, term_own, term_other, full_ref):
    half = lax.axis_index("core")
    lane = lanes_of((40, 128))
    edges = [unpacked_edge(sent_ref[facet, 72:80]) for facet in range(8)]
    for facet in range(8):
        value = sent_ref[facet, 32:72]
        if facet > 0:
            value = value + jnp.where(lane < HALO, edges[facet - 1], 0.0)
        if facet < 7:
            value = value + jnp.where(lane >= 128 - HALO, edges[facet + 1], 0.0)
        full_ref[facet] = value
    for i in range(4):
        cols = slice(128 * i, 128 * i + 128)
        image_own[:, cols] = sent_ref[4 * half + i, 0:32]
        image_other[:, cols] = sent_ref[4 - 4 * half + i, 0:32]
        term_own[:, cols] = full_ref[4 * half + i]
        term_other[:, cols] = full_ref[4 - 4 * half + i]


def split(sent):
    return pl.pallas_call(
        split_kernel,
        in_specs=[VMEM],
        out_specs=[VMEM] * 4,
        out_shape=[
            jax.ShapeDtypeStruct((32, 512), F32),
            sent_out(32, 512),
            sent_out(40, 512),
            sent_out(40, 512),
        ],
        scratch_shapes=[pltpu.VMEM((8, 40, 128), F32)],
        compiler_params=params(),
        cost_estimate=cost(1),
        name="split",
    )(sent)


def rows_kernel(own_ref, theirs_ref, out_ref):
    half = lax.axis_index("core")
    for ref, start in ((own_ref, 32 * half), (theirs_ref, 32 - 32 * half)):
        out_ref[pl.ds(pl.multiple_of(start, 32), 32)] = ref[...]


def join_rows(own, theirs):
    return pl.pallas_call(
        rows_kernel,
        in_specs=[VMEM, VMEM],
        out_specs=VMEM,
        out_shape=jax.ShapeDtypeStruct((64, 512), F32),
        compiler_params=params(),
        cost_estimate=cost(1),
        name="join_rows",
    )(own, theirs)


def join_kernel(own_ref, theirs_ref, out_ref):
    half = lax.axis_index("core")
    out_ref[...] = jnp.zeros((72, 512), F32)
    for ref, start in ((own_ref, 32 * half), (theirs_ref, 32 - 32 * half)):
        rows = pl.ds(pl.multiple_of(start, 32), 40)
        out_ref[rows] += ref[...]


def join(own, theirs):
    return pl.pallas_call(
        join_kernel,
        in_specs=[VMEM, VMEM],
        out_specs=VMEM,
        out_shape=jax.ShapeDtypeStruct((72, 512), F32),
        compiler_params=params(),
        cost_estimate=cost(1),
        name="join",
    )(in_hbm(own), theirs)


def spread_rows(scal_ref, q, step, ch, field, padded_ref, total_ref):
    padded_ref[ch, 8:40] = field
    low, mid, high = HALO + step, HALO, HALO - step
    value = (
        scal_ref[q, 0] * padded_ref[ch, low : low + 40]
        + scal_ref[q, 1] * padded_ref[ch, mid : mid + 40]
        + scal_ref[q, 2] * padded_ref[ch, high : high + 40]
    )
    for e in range(3):
        total_ref[SHIFTS.index((e - 1) * step), ch] += scal_ref[q, 3 + e] * value


def clear(padded_ref, total_ref):
    for ch in range(8):
        padded_ref[ch, 0:8] = jnp.zeros((8, 128), F32)
        padded_ref[ch, 40:48] = jnp.zeros((8, 128), F32)
        for d in range(7):
            total_ref[d, ch] = jnp.zeros((40, 128), F32)


def shift_all(total_ref, ch):
    lane = lanes_of((40, 128))
    main = total_ref[0, ch]
    edge = jnp.zeros((40, 128), F32)
    for d, col in enumerate(SHIFTS):
        if col:
            turned = pltpu.roll(total_ref[d, ch], col % 128, 1)
            inside = (lane >= col) if col > 0 else (lane < 128 + col)
            main = main + jnp.where(inside, turned, 0.0)
            edge = edge + jnp.where(inside, 0.0, turned)
    return main, edge


def shifted_columns(field_ref, turned_ref):
    lane = lanes_of((40, 128))

    @pl.loop(0, 8)
    def channel(ch):
        main = field_ref[ch, :40]
        edge = field_ref[ch, 40:]
        for d, col in enumerate(SHIFTS):
            if col:
                inside = (lane < 128 - col) if col > 0 else (lane >= -col)
                turned_ref[d, ch] = jnp.where(
                    inside, pltpu.roll(main, -col % 128, 1), pltpu.roll(edge, -col % 128, 1)
                )
            else:
                turned_ref[d, ch] = main


def each_level(scal_ref, q, work):
    for level, step in enumerate(STEPS):
        pl.when(scal_ref[q, 7] == F32(level + 1))(functools.partial(work, step))


def shrink(scal_ref, q, at, dual_ref, turned_ref, out_ref, after=None):
    def at_level(step):
        low, mid, high = (SHIFTS.index(s) for s in (-step, 0, step))
        squares = jnp.zeros((32, 128), F32)
        for ch in range(8):
            across = (
                scal_ref[q, 3] * turned_ref[low, ch]
                + scal_ref[q, 4] * turned_ref[mid, ch]
                + scal_ref[q, 5] * turned_ref[high, ch]
            )
            value = (
                scal_ref[q, 0] * across[HALO - step : HALO - step + 32]
                + scal_ref[q, 1] * across[HALO : HALO + 32]
                + scal_ref[q, 2] * across[HALO + step : HALO + step + 32]
            )
            raised = dual_ref[at, ch] + 0.5 * value
            out_ref[at, ch] = raised
            squares = squares + raised * raised
        limit = scal_ref[q, 6]
        scale = limit / jnp.maximum(jnp.sqrt(squares), limit)
        for ch in range(8):
            value = out_ref[at, ch] * scale
            out_ref[at, ch] = value
            if after is not None:
                after(step, ch, value)

    each_level(scal_ref, q, at_level)


class Scalars:
    def __init__(self, filters_ref, level_ref):
        self.filters_ref = filters_ref
        self.level_ref = level_ref

    def __getitem__(self, at):
        q, column = at
        if column == 7:
            return self.level_ref[q].astype(F32)
        return self.filters_ref[column % 3, column // 3, q]


def start_kernel(filters_ref, level_ref, image_ref, dual_ref, out_ref, padded_ref, total_ref):
    step_index = pl.program_id(0)
    scal_ref = Scalars(filters_ref, level_ref)

    @pl.when(step_index == 0)
    def first():
        clear(padded_ref, total_ref)

    @pl.loop(0, 3)
    def basis(i):
        q = 3 * step_index + i

        def at_level(step):
            for ch in range(8):
                spread_rows(scal_ref, q, step, ch, dual_ref[i, ch], padded_ref, total_ref)

        each_level(scal_ref, q, at_level)

    @pl.when(step_index == 2)
    def final():
        for ch in range(8):
            main, edge = shift_all(total_ref, ch)
            out_ref[ch, 0:32] = image_ref[ch]
            out_ref[ch, 32:72] = main
            out_ref[ch, 72:80] = packed_edge(edge)


TURNED = pltpu.VMEM((7, 8, 40, 128), F32)
FIELD = pltpu.VMEM((8, 80, 128), F32)
PADDED = pltpu.VMEM((8, 48, 128), F32)
THIRD = pl.BlockSpec((3, 8, 32, 128), lambda i: (i, 0, 0, 0))


def whole(*shape):
    return pl.BlockSpec(shape, lambda i: (0,) * len(shape))


def start(filters, levels, image, dual):
    return pl.pallas_call(
        start_kernel,
        grid=(3,),
        in_specs=[SMEM, SMEM, whole(8, 32, 128), THIRD],
        out_specs=whole(8, 80, 128),
        out_shape=sent_out(8, 80, 128),
        scratch_shapes=[PADDED, TURNED],
        compiler_params=params(),
        cost_estimate=cost(4),
        name="start",
    )(filters, in_hbm(levels), in_hbm(image), in_hbm(dual))


def middle_kernel(scal_ref, before_ref, pair_ref, dual_ref, dual_out, part_out, right_out, left_out,
                  now_out, field_ref, turned_ref, padded_ref, total_ref):
    step_index = pl.program_id(0)

    @pl.when(step_index == 0)
    def first():
        for ch in range(8):
            main = pair_ref[ch, :40]
            now_out[ch, :40] = main
            now = 2.0 * main
            field_ref[ch, 4:36] = now[4:36] - before_ref[ch]
            outer = pair_ref[ch, 56:64]
            field_ref[ch, 0:4] = now[0:4] - outer[0:4]
            field_ref[ch, 36:40] = now[36:40] - outer[4:8]
            edge = unpacked_edge(pair_ref[ch, 40:48])
            now_out[ch, 40:] = edge
            field_ref[ch, 40:] = 2.0 * edge - unpacked_edge(pair_ref[ch, 48:56])
        shifted_columns(field_ref, turned_ref)
        clear(padded_ref, total_ref)

    @pl.loop(0, 3)
    def basis(i):
        q = 3 * step_index + i

        def after(step, ch, value):
            spread_rows(scal_ref, q, step, ch, value, padded_ref, total_ref)

        shrink(scal_ref, q, i, dual_ref, turned_ref, dual_out, after)

    @pl.when(step_index == 2)
    def final():
        lane = lanes_of((40, 128))
        for ch in range(8):
            main, edge = shift_all(total_ref, ch)
            part_out[ch, :40] = main
            part_out[ch, 40:] = edge
            right_out[ch] = jnp.where(lane >= 128 - HALO, main, edge)
            left_out[ch] = jnp.where(lane < HALO, main, edge)


def middle(scal, dual, before, pair):
    side = jax.ShapeDtypeStruct((8, 40, 128), F32)
    field = sent_out(8, 80, 128)
    return pl.pallas_call(
        middle_kernel,
        grid=(3,),
        in_specs=[SMEM, whole(8, 32, 128), whole(8, 64, 128), THIRD],
        out_specs=[THIRD, whole(8, 80, 128)] + [whole(8, 40, 128)] * 2 + [whole(8, 80, 128)],
        out_shape=[sent_out(NBASIS, 8, 32, 128), field, side, side, field],
        scratch_shapes=[FIELD, TURNED, PADDED, TURNED],
        compiler_params=params(20),
        cost_estimate=cost(7),
        name="middle",
    )(scal, in_hbm(before), pair, in_hbm(dual))


def last_kernel(scal_ref, now_ref, part_ref, above_ref, below_ref, gradient_ref, dual_ref,
                image_out, dual_out, field_ref, turned_ref):
    step_index = pl.program_id(0)

    @pl.when(step_index == 0)
    def first():
        chip_row, facet = where_am_i()[2:]
        lane = lanes_of((40, 128))
        row = lax.broadcasted_iota(jnp.int32, (40, 128), 0) + (32 * chip_row - HALO)
        in_rows = (row >= 0) & (row < 512)
        in_edge = ((lane < HALO) & (facet < 7)) | ((lane >= 128 - HALO) & (facet > 0))
        for ch in range(8):
            for start, keep in ((0, in_rows), (40, in_rows & in_edge)):
                which = start // 40
                gradient = unpacked_edge(gradient_ref[ch, 40:]) if which else gradient_ref[ch, :40]
                field_ref[ch, start : start + 40] = part_ref[ch, start : start + 40] + gradient
                field_ref[ch, start : start + 8] += above_ref[ch, which]
                field_ref[ch, start + 32 : start + 40] += below_ref[ch, which]
                now = now_ref[ch, start : start + 40]
                value = jnp.maximum(now - 0.5 * field_ref[ch, start : start + 40], 0.0)
                value = jnp.where(keep, value, 0.0)
                if start == 0:
                    image_out[ch] = value[HALO : HALO + 32]
                field_ref[ch, start : start + 40] = 2.0 * value - now
        shifted_columns(field_ref, turned_ref)

    @pl.loop(0, 3)
    def basis(i):
        shrink(scal_ref, 3 * step_index + i, i, dual_ref, turned_ref, dual_out)


def last(scal, dual, now, part, above, below, gradient):
    field, side = whole(8, 80, 128), whole(8, 2, 8, 128)
    return pl.pallas_call(
        last_kernel,
        grid=(3,),
        in_specs=[SMEM, field, field, side, side, whole(8, 48, 128), THIRD],
        out_specs=[whole(8, 32, 128), THIRD],
        out_shape=[
            jax.ShapeDtypeStruct((8, 32, 128), F32),
            jax.ShapeDtypeStruct((NBASIS, 8, 32, 128), F32),
        ],
        scratch_shapes=[FIELD, TURNED],
        compiler_params=params(20),
        cost_estimate=cost(4),
        name="last",
    )(scal, now, part, above, below, gradient, dual)


def swapped(value):
    return lax.ppermute(value, "core", [(0, 1), (1, 0)])


def gathered(value):
    return gathered_x(value) + gathered_x(across_y(value))


def to_chips(pieces):
    arrived = [pieces[0]]
    for i in range(1, 8):
        route = [
            (4 * y + x, 4 * (y ^ (i // 4)) + (x + i) % 4) for y in range(2) for x in range(4)
        ]
        arrived.append(lax.ppermute(pieces[i], CHIPS, route))
    return arrived


def across_y(value):
    return lax.ppermute(value, "y", [(0, 1), (1, 0)])


def along_x(value, step):
    return lax.ppermute(value, "x", [(i, (i + step) % 4) for i in range(4)])


def gathered_x(value):
    return [value] + [along_x(value, -ahead) for ahead in (1, 2, 3)]


def neighbours(value, axis, count, step):
    return lax.ppermute(
        value, axis, [(i, i + step) for i in range(count) if 0 <= i + step < count]
    )


def half_of(value, half, size, dim):
    return lax.dynamic_slice_in_dim(value, half * size, size, dim)


def per_device(
    sky_image,
    dual_coefs,
    phase_screen,
    grid_rows,
    grid_weight,
    visibilities,
    filters,
    level_counts,
    radius,
):
    half = lax.axis_index("core")
    scal = jnp.concatenate(
        [filters.reshape(NBASIS, 6), radius[:, None], level_counts[:, None].astype(F32)], axis=1
    )

    packed = start(filters.transpose(2, 1, 0), level_counts, sky_image, dual_coefs)
    sent = lax.all_to_all(packed, "chan", 0, 0, tiled=True)

    weight_own = grid_weight[0, 0]
    weight_other, phase = lax.optimization_barrier((swapped(weight_own), phase_screen[0, 0]))
    phase_other = half_of(phase, 1 - half, 512, 1)
    data_own = visibilities[0, 0].reshape(128, 256)
    data = jnp.stack([data_own, swapped(data_own)])
    rows_own = grid_rows[0, 0]
    rows_other = swapped(rows_own.astype(F32)).astype(jnp.int32)
    left, right = tables(jnp.stack([rows_own, rows_other]))
    grid = gridding(weight_own, weight_other)
    sent, grid, phase_other = lax.optimization_barrier((sent, grid, phase_other))
    trig = screens(phase, swapped(phase_other))

    own, other, term_own, term_other = split(sent)
    strip = join_rows(own, swapped(other))
    pieces = gathered(strip)
    extra = join(term_own, swapped(term_other))
    pieces, extra, data = lax.optimization_barrier((pieces, extra, data))

    seen, seen_copy, window = forward(pieces, trig, left, grid, True)
    sent = backward(seen_copy, swapped(seen), data, grid, right, trig, extra)
    sent = to_chips(sent)
    own, other, core = update(sent, window)

    pieces = gathered(core)
    packed = pair_to_facets(own, swapped(other))
    packed, pieces[4] = lax.optimization_barrier((packed, pieces[4]))
    pair = lax.all_to_all(packed, "chan", 0, 0, tiled=True)
    seen, seen_copy = forward(pieces, trig, left, grid, False)
    dual, part, to_right, to_left, now = middle(scal, dual_coefs, sky_image, pair)
    sent = backward(seen_copy, swapped(seen), data, grid, right, trig)
    windows = total_windows(lax.all_to_all(sent, CHIPS, 0, 0, tiled=True))
    from_left = neighbours(to_right, "chan", 8, 1)
    from_right = neighbours(to_left, "chan", 8, -1)
    packed = to_facets(*windows)
    from_left, from_right = lax.optimization_barrier((from_left, from_right, packed))[:2]
    lane = lanes_of((8, 40, 128))
    main = part[:, :40] + jnp.where(lane < HALO, from_left, 0.0)
    main = main + jnp.where(lane >= 128 - HALO, from_right, 0.0)
    edge = part[:, 40:] + jnp.where(lane >= 128 - HALO, from_left, 0.0)
    edge = edge + jnp.where(lane < HALO, from_right, 0.0)
    both = jnp.stack([main, edge], axis=1)
    above = neighbours(both[:, :, 32:], ("y", "x", "core"), 16, 1)
    below = neighbours(both[:, :, :8], ("y", "x", "core"), 16, -1)
    gradient = lax.all_to_all(packed, "chan", 0, 0, tiled=True)
    return tuple(last(scal, dual, now, both.reshape(8, 80, 128), above, below, gradient))


def solution(mesh):
    fine = Mesh(mesh.devices.reshape(8, 2, 4, 2), ("chan", "y", "x", "core"))
    rows = ("y", "x", "core")
    placed = (
        P(None, rows, "chan"),
        P(None, None, rows, "chan"),
        P("chan", rows, None, None),
        P("chan", rows, None),
        P("chan", rows, None, None),
        P("chan", rows, None, None, None),
        P(),
        P(),
        P(),
    )
    return jax.shard_map(
        per_device,
        mesh=fine,
        in_specs=placed,
        out_specs=(P(None, rows, "chan"), P(None, None, rows, "chan")),
        check_vma=False,
    )
```

```python
import functools
import math

import jax
import jax.numpy as jnp
import ml_dtypes
import numpy as np
from jax import lax
from jax.experimental import pallas as pl
from jax.experimental.pallas import tpu as pltpu
from jax.sharding import Mesh
from jax.sharding import PartitionSpec as P

NBASIS = 9
HALO = 4
CHIPS = ("y", "x")
F32 = jnp.float32
BF16 = jnp.bfloat16
STEPS = (1, 2, 4)
SHIFTS = (0, -1, 1, -2, 2, -4, 4)
MIB = 1024 * 1024
SMEM = pl.BlockSpec(memory_space=pltpu.SMEM)
VMEM = pl.BlockSpec(memory_space=pltpu.VMEM)
ANY = pl.BlockSpec(memory_space=pltpu.HBM)


def params(size=16):
    return pltpu.CompilerParams(vmem_limit_bytes=size * MIB)


def where_am_i():
    half = lax.axis_index("core")
    chip = lax.axis_index("y") * 4 + lax.axis_index("x")
    return half, chip, 2 * chip + half, lax.axis_index("chan")


def cost(us):
    return pl.CostEstimate(flops=0, bytes_accessed=int(us * 3.0e6), transcendentals=0)


def sent_out(*shape):
    return pltpu.HBM(shape, F32)


def kept(shape, kind=F32):
    return pltpu.VMEM(shape, kind)


def in_hbm(value):
    return pltpu.with_memory_space_constraint(value, pltpu.HBM)


def chip_of(other_y, ahead):
    y = lax.axis_index("y")
    return 4 * ((1 - y) if other_y else y) + ((lax.axis_index("x") + ahead) & 3)


def parts(value):
    high = value.astype(BF16)
    return high, (value - high.astype(F32)).astype(BF16)


def dot(left, right):
    return jnp.dot(left, right, preferred_element_type=F32)


def dot_t(left, right):
    return lax.dot_general(left, right, (((1,), (1,)), ((), ())), preferred_element_type=F32)


def sincos(angle):
    y = 0.5 * angle
    z = y * y
    s = F32(2.6050929582509915e-06)
    for a in (-0.00019809011067269285, 0.008333050086782038, -0.16666657944392363, 0.9999999956966753):
        s = s * z + F32(a)
    s = s * y
    c = F32(-2.6050510628158867e-07)
    for a in (
        2.476010151557824e-05,
        -0.0013888360127752544,
        0.041666636147634536,
        -0.4999999935511792,
        0.9999999997790222,
    ):
        c = c * z + F32(a)
    return 2.0 * s * c, 1.0 - 2.0 * s * s


def rounded(value):
    return ((value * 32767.0 + 32768.5).astype(jnp.int32) - 32768).astype(jnp.int16)


def widened(value):
    return value.astype(jnp.int32).astype(F32)


def screens_kernel(other_ref, phase_hbm, out_ref, own_ref, sems):
    cols = pl.ds(pl.multiple_of(512 * lax.axis_index("core"), 512), 512)
    copies = [
        pltpu.make_async_copy(
            phase_hbm.at[pl.ds(128 * i, 128), cols], own_ref.at[pl.ds(128 * i, 128)], sems.at[i]
        )
        for i in range(4)
    ]
    for copy in copies:
        copy.start()

    def fill(b, ref, start):
        at = pl.ds(pl.multiple_of(start, 32), 32)
        s, c = sincos(ref[at])
        for part in range(2):
            cols = slice(256 * part, 256 * part + 256)
            out_ref[b, part, 0, at] = rounded(c[:, cols])
            out_ref[b, part, 1, at] = rounded(s[:, cols])

    pl.loop(0, 512, step=32)(functools.partial(fill, 1, other_ref))
    for i in range(4):
        copies[i].wait()
        pl.loop(128 * i, 128 * i + 128, step=32)(functools.partial(fill, 0, own_ref))


def screens(phase, other):
    return pl.pallas_call(
        screens_kernel,
        in_specs=[VMEM, ANY],
        out_specs=VMEM,
        out_shape=kept((2, 2, 2, 512, 256), jnp.int16),
        scratch_shapes=[pltpu.VMEM((512, 512), F32), pltpu.SemaphoreType.DMA((4,))],
        compiler_params=params(),
        cost_estimate=cost(4),
        name="screens",
    )(other, in_hbm(phase))


def tables_kernel(gcol_ref, grow_ref, left_ref, right_ref):
    size = 512
    for b in range(2):
        for turned, g_ref, out_ref in ((0, gcol_ref, left_ref), (1, grow_ref, right_ref)):
            shape = (size, 128) if turned else (128, size)
            n = lax.broadcasted_iota(jnp.int32, shape, 0 if turned else 1)
            picked = lax.broadcasted_iota(jnp.int32, shape, 1 if turned else 0)
            index = (g_ref[b] * n) & (size - 1)
            index = jnp.where(index >= size // 2, index - size, index)
            s, c = sincos(index.astype(F32) * F32(2.0 * math.pi / size))
            high, low = parts(jnp.where(picked < 64, c, -s) * F32(1.0 / math.sqrt(size)))
            if turned:
                out_ref[b, :, :128] = high
                out_ref[b, :, 128:] = low
            else:
                out_ref[b, :128, :] = high
                out_ref[b, 128:, :] = low


def tables(rows_both):
    doubled = jnp.concatenate([rows_both, rows_both], axis=1)
    return pl.pallas_call(
        tables_kernel,
        in_specs=[VMEM, VMEM],
        out_specs=[VMEM, VMEM],
        out_shape=[
            pltpu.HBM((2, 256, 512), BF16),
            pltpu.HBM((2, 512, 256), BF16),
        ],
        compiler_params=params(),
        cost_estimate=cost(2),
        name="tables",
    )(doubled[:, :, None], doubled[:, None, :])


def gridding_kernel(own_ref, other_ref, table_ref, turn_ref, out_ref, first_ref, second_ref):
    half = lax.axis_index("core")
    sign = jnp.where(half == 1, F32(-1.0), F32(1.0))
    table = table_ref[...]
    for b, ref in enumerate((own_ref, other_ref)):
        turned = []
        first_ref[...] = ref[:, :128]
        second_ref[...] = ref[:, 128:]
        for q in range(4):
            rows = pl.ds(q, 256, stride=4)
            high, low = parts(jnp.concatenate([first_ref[rows], second_ref[rows]], axis=1))
            value = dot(table, high)
            real = value[0:256] + value[256:512]
            imag = value[512:768] + value[768:1024]
            value = dot(table[0:256], low)
            real = real + value
            value = dot(table[512:768], low)
            imag = imag + value
            if q:
                cos, sin = turn_ref[:, 2 * q : 2 * q + 1], turn_ref[:, 2 * q + 1 : 2 * q + 2]
                if q & 1:
                    cos, sin = cos * sign, sin * sign
                real, imag = cos * real + sin * imag, cos * imag - sin * real
            turned.append((real, imag))
        even = [turned[0][i] + turned[2][i] for i in range(2)]
        odd = [turned[1][i] + turned[3][i] for i in range(2)]
        near = [even[i] + odd[i] for i in range(2)]
        even = [turned[0][i] - turned[2][i] for i in range(2)]
        odd = [turned[1][i] - turned[3][i] for i in range(2)]
        far = [even[0] + odd[1], even[1] - odd[0]]
        for cols, values in enumerate((near, far)):
            for part in range(2):
                high, low = parts(values[part])
                out_ref[b, cols, part, 0] = high
                out_ref[b, cols, part, 1] = low


def column_table():
    angle = (np.arange(256)[:, None] * np.arange(256)[None, :] % 256) * (2.0 * np.pi / 256)
    out = np.zeros((4, 256, 256), ml_dtypes.bfloat16)
    for part, value in enumerate((np.cos(angle) / 32.0, -np.sin(angle) / 32.0)):
        high = value.astype(ml_dtypes.bfloat16)
        out[2 * part] = high
        out[2 * part + 1] = (value - high.astype(np.float64)).astype(ml_dtypes.bfloat16)
    return out.reshape(1024, 256)


def turns():
    out = np.zeros((256, 8), np.float32)
    for q in range(4):
        angle = np.arange(256) * q * (2.0 * np.pi / 1024)
        out[:, 2 * q] = np.cos(angle)
        out[:, 2 * q + 1] = np.sin(angle)
    return out


def gridding(own, other):
    return pl.pallas_call(
        gridding_kernel,
        in_specs=[VMEM] * 4,
        out_specs=VMEM,
        out_shape=pltpu.HBM((2, 2, 2, 2, 256, 256), BF16),
        scratch_shapes=[pltpu.VMEM((1024, 128), F32)] * 2,
        compiler_params=params(),
        cost_estimate=cost(3),
        name="gridding",
    )(own, other, column_table(), turns())


def thrice(left, high, low, form):
    count = left.shape[0] // 2
    both = form(left, high)
    return both[:count] + both[count:] + form(left[:count], low)


def fetch(table_hbm, grid_hbm, table_ref, grid_ref, sems, order):
    copies = {}
    for i, key in enumerate(order):
        source, target = (table_hbm, table_ref) if len(key) == 1 else (grid_hbm, grid_ref)
        copies[key] = pltpu.make_async_copy(source.at[key], target.at[key], sems.at[i])
        copies[key].start()
    return copies


FETCHED = [
    pltpu.VMEM((2, 2, 2, 2, 256, 256), BF16),
    pltpu.SemaphoreType.DMA((6,)),
]


def forward_kernel(*refs, windows):
    pieces, (trig_ref, left_hbm, grid_hbm, out_ref, copy_ref) = refs[: -9 - windows], refs[-9 - windows : -4 - windows]
    image_ref, left_ref, grid_ref, sems = refs[-4:]
    order = [(0,), (0, 0), (0, 1), (1,), (1, 0), (1, 1)]
    copies = fetch(left_hbm, grid_hbm, left_ref, grid_ref, sems, order)
    for i, ref in enumerate(pieces):
        start = pl.multiple_of(64 * chip_of(i // 4, i % 4) + 8, 8)
        image_ref[pl.ds(start, 64)] = ref[...]
    if windows:
        image_ref[0:8] = jnp.zeros((8, 512), F32)
        image_ref[520:528] = jnp.zeros((8, 512), F32)
        refs[-5][...] = image_ref[pl.ds(pl.multiple_of(64 * chip_of(0, 0), 64), 80)][4:76]
    for b in range(2):
        total = None
        copies[(b,)].wait()
        left = left_ref[b]
        for part in range(2):
            image = image_ref[8:520, 256 * part : 256 * part + 256] * F32(1.0 / 32767.0)
            from_real = thrice(left, *parts(widened(trig_ref[b, part, 0]) * image), dot)
            from_imag = thrice(left, *parts(widened(trig_ref[b, part, 1]) * image), dot)
            spectrum = jnp.concatenate(
                [from_real[:64] - from_imag[64:], from_imag[:64] + from_real[64:]], axis=0
            )
            spectrum = jnp.concatenate(parts(spectrum), axis=0)
            copies[(b, part)].wait()
            by_real = thrice(spectrum, grid_ref[b, part, 0, 0], grid_ref[b, part, 0, 1], dot)
            by_imag = thrice(spectrum, grid_ref[b, part, 1, 0], grid_ref[b, part, 1, 1], dot)
            seen = jnp.concatenate(
                [by_real[:64] - by_imag[64:], by_imag[:64] + by_real[64:]], axis=0
            )
            total = seen if total is None else total + seen
        out_ref[b] = total
        copy_ref[b] = total


def forward(pieces, trig, left, grid, windows):
    shapes = [jax.ShapeDtypeStruct((2, 128, 256), F32)] * 2
    if windows:
        shapes = shapes + [jax.ShapeDtypeStruct((72, 512), F32)]
    return pl.pallas_call(
        functools.partial(forward_kernel, windows=windows),
        in_specs=[VMEM] * (len(pieces) + 1) + [ANY] * 2,
        out_specs=[VMEM] * len(shapes),
        out_shape=shapes,
        scratch_shapes=[pltpu.VMEM((528, 512), F32), pltpu.VMEM((2, 256, 512), BF16)] + FETCHED,
        compiler_params=params(20),
        cost_estimate=cost(5),
        name="forward",
    )(*pieces, trig, in_hbm(left), in_hbm(grid))


def backward_kernel(mine_ref, theirs_ref, data_ref, trig_ref, *rest):
    extra_ref = rest[0] if len(rest) == 15 else None
    right_hbm, grid_hbm, *outs = rest[-7:-4] if extra_ref is None else rest[-14:-4]
    total_ref, right_ref, grid_ref, sems = rest[-4:]
    order = [(0, 0), (0,), (1, 0), (1,), (0, 1), (1, 1)]
    copies = fetch(right_hbm, grid_hbm, right_ref, grid_ref, sems, order)
    total_ref[0:8] = jnp.zeros((8, 512), F32)
    total_ref[512:520] = jnp.zeros((8, 512), F32)
    misfits = [
        jnp.concatenate(parts(mine_ref[b] + theirs_ref[1 - b] - data_ref[b]), axis=0) for b in range(2)
    ]
    for half in range(2):
        cols = slice(256 * half, 256 * half + 256)
        total = None
        for b in range(2):
            copies[(b, half)].wait()
            by_real = thrice(misfits[b], grid_ref[b, half, 0, 0], grid_ref[b, half, 0, 1], dot_t)
            by_imag = thrice(misfits[b], grid_ref[b, half, 1, 0], grid_ref[b, half, 1, 1], dot_t)
            real = by_real[:64] + by_imag[64:]
            imag = by_real[64:] - by_imag[:64]
            spread = jnp.concatenate(
                [jnp.concatenate([real, imag], axis=1), jnp.concatenate([imag, -real], axis=1)],
                axis=0,
            )
            high, low = parts(spread * F32(1.0 / 32767.0))
            if half == 0:
                copies[(b,)].wait()
            right = right_ref[b]
            pulled = dot(right, jnp.concatenate([high, high], axis=0)) + dot(right[:, :128], low)
            part = widened(trig_ref[b, half, 0]) * pulled[:, :256]
            part = part + widened(trig_ref[b, half, 1]) * pulled[:, 256:]
            total = part if total is None else total + part
        total_ref[4:516, cols] = total
    if extra_ref is not None:
        rows = pl.ds(pl.multiple_of(64 * chip_of(0, 0), 64), 72)
        total_ref[rows] += extra_ref[...]
    if extra_ref is None:
        for chip in range(8):
            outs[0][chip] = total_ref[64 * chip : 64 * chip + 72]
    else:
        for i, ref in enumerate(outs):
            ref[...] = total_ref[pl.ds(pl.multiple_of(64 * chip_of(i // 4, i % 4), 64), 72)]


def backward(mine, theirs, data, grid, right, trig, extra=None):
    args = [mine, theirs, data, trig] + ([] if extra is None else [extra])
    pieces = [jax.ShapeDtypeStruct((72, 512), F32)] * 8
    return pl.pallas_call(
        backward_kernel,
        in_specs=[VMEM] * len(args) + [ANY] * 2,
        out_specs=VMEM if extra is None else [VMEM] * 8,
        out_shape=sent_out(8, 72, 512) if extra is None else pieces,
        scratch_shapes=[pltpu.VMEM((520, 512), F32), pltpu.VMEM((2, 512, 256), BF16)] + FETCHED,
        compiler_params=params(20),
        cost_estimate=cost(5),
        name="backward",
    )(*args, in_hbm(right), in_hbm(grid))


def sum_of(refs):
    total = refs[0][...]
    for ref in refs[1:]:
        total = total + ref[...]
    return total


def update_kernel(*refs):
    image_ref, own_ref, other_ref, core_ref, scratch_ref = refs[8:]
    half, chip = where_am_i()[:2]
    total = sum_of(refs[:8])
    row = lax.broadcasted_iota(jnp.int32, total.shape, 0) + (64 * chip - HALO)
    value = jnp.maximum(image_ref[...] - 0.5 * total, 0.0)
    scratch_ref[...] = jnp.where((row >= 0) & (row < 512), value, 0.0)
    for window_ref, start in ((own_ref, 32 * half), (other_ref, 32 - 32 * half)):
        rows = pl.ds(pl.multiple_of(start, 32), 40)
        window_ref[0] = scratch_ref[rows]
        window_ref[1] = image_ref[rows]
    core_ref[...] = scratch_ref[HALO : HALO + 64]


def update(sent, image):
    window = jax.ShapeDtypeStruct((2, 40, 512), F32)
    return pl.pallas_call(
        update_kernel,
        in_specs=[VMEM] * 9,
        out_specs=[VMEM] * 3,
        out_shape=[window, window, jax.ShapeDtypeStruct((64, 512), F32)],
        scratch_shapes=[pltpu.VMEM((72, 512), F32)],
        compiler_params=params(),
        cost_estimate=cost(1),
        name="update",
    )(*sent, image)


def total_kernel(sent_ref, own_ref, other_ref, scratch_ref):
    half = lax.axis_index("core")
    scratch_ref[...] = sum_of([sent_ref.at[source] for source in range(8)])
    own_ref[...] = scratch_ref[pl.ds(pl.multiple_of(32 * half, 32), 40)]
    other_ref[...] = scratch_ref[pl.ds(pl.multiple_of(32 - 32 * half, 32), 40)]


def total_windows(sent):
    window = jax.ShapeDtypeStruct((40, 512), F32)
    return pl.pallas_call(
        total_kernel,
        in_specs=[VMEM],
        out_specs=[VMEM] * 2,
        out_shape=[window, window],
        scratch_shapes=[pltpu.VMEM((72, 512), F32)],
        compiler_params=params(),
        cost_estimate=cost(1),
        name="total_windows",
    )(sent)


def lanes_of(shape):
    return lax.broadcasted_iota(jnp.int32, shape, len(shape) - 1)


def packed_edge(edge):
    lane = lanes_of((8, 128))
    out = jnp.zeros((8, 128), F32)
    for g in range(5):
        turned = pltpu.roll(edge[8 * g : 8 * g + 8], 8 * g + HALO, 1)
        out = jnp.where((lane >= 8 * g) & (lane < 8 * g + 8), turned, out)
    return out


def unpacked_edge(packed):
    lane = lanes_of((40, 128))
    turned = [pltpu.roll(packed, 128 - HALO - 8 * g, 1) for g in range(5)]
    inside = (lane < HALO) | (lane >= 128 - HALO)
    return jnp.where(inside, jnp.concatenate(turned, axis=0), 0.0)


def to_facets_kernel(own_ref, theirs_ref, out_ref, full_ref):
    half = lax.axis_index("core")
    full_ref[0] = jnp.zeros((40, 128), F32)
    full_ref[9] = jnp.zeros((40, 128), F32)
    for i in range(4):
        full_ref[1 + 4 * half + i] = own_ref[:, 128 * i : 128 * i + 128]
        full_ref[5 - 4 * half + i] = theirs_ref[:, 128 * i : 128 * i + 128]
    lane = lanes_of((40, 128))
    for facet in range(8):
        out_ref[facet, :40] = full_ref[facet + 1]
        out_ref[facet, 40:] = packed_edge(
            jnp.where(lane < HALO, full_ref[facet + 2], full_ref[facet])
        )


def to_facets(own, other):
    theirs = swapped(other)
    return pl.pallas_call(
        to_facets_kernel,
        in_specs=[VMEM, VMEM],
        out_specs=VMEM,
        out_shape=sent_out(8, 48, 128),
        scratch_shapes=[pltpu.VMEM((10, 40, 128), F32)],
        compiler_params=params(),
        cost_estimate=cost(1),
        name="to_facets",
    )(own, theirs)


def pair_kernel(own_ref, theirs_ref, out_ref, full_ref):
    half = lax.axis_index("core")
    for which in range(2):
        full_ref[which, 0] = jnp.zeros((40, 128), F32)
        full_ref[which, 9] = jnp.zeros((40, 128), F32)
        for i in range(4):
            full_ref[which, 1 + 4 * half + i] = own_ref[which, :, 128 * i : 128 * i + 128]
            full_ref[which, 5 - 4 * half + i] = theirs_ref[which, :, 128 * i : 128 * i + 128]
    lane = lanes_of((40, 128))
    row = lax.broadcasted_iota(jnp.int32, (8, 128), 0)
    for facet in range(8):
        out_ref[facet, :40] = full_ref[0, facet + 1]
        for which in range(2):
            out_ref[facet, 40 + 8 * which : 48 + 8 * which] = packed_edge(
                jnp.where(lane < HALO, full_ref[which, facet + 2], full_ref[which, facet])
            )
        out_ref[facet, 56:64] = jnp.where(
            row < HALO, full_ref[1, facet + 1, 0:8], full_ref[1, facet + 1, 32:40]
        )


def pair_to_facets(own, theirs):
    return pl.pallas_call(
        pair_kernel,
        in_specs=[VMEM, VMEM],
        out_specs=VMEM,
        out_shape=sent_out(8, 64, 128),
        scratch_shapes=[pltpu.VMEM((2, 10, 40, 128), F32)],
        compiler_params=params(),
        cost_estimate=cost(1),
        name="pair_to_facets",
    )(own, theirs)


def split_kernel(sent_ref, image_own, image_other, term_own, term_other, full_ref):
    half = lax.axis_index("core")
    lane = lanes_of((40, 128))
    edges = [unpacked_edge(sent_ref[facet, 72:80]) for facet in range(8)]
    for facet in range(8):
        value = sent_ref[facet, 32:72]
        if facet > 0:
            value = value + jnp.where(lane < HALO, edges[facet - 1], 0.0)
        if facet < 7:
            value = value + jnp.where(lane >= 128 - HALO, edges[facet + 1], 0.0)
        full_ref[facet] = value
    for i in range(4):
        cols = slice(128 * i, 128 * i + 128)
        image_own[:, cols] = sent_ref[4 * half + i, 0:32]
        image_other[:, cols] = sent_ref[4 - 4 * half + i, 0:32]
        term_own[:, cols] = full_ref[4 * half + i]
        term_other[:, cols] = full_ref[4 - 4 * half + i]


def split(sent):
    return pl.pallas_call(
        split_kernel,
        in_specs=[VMEM],
        out_specs=[VMEM] * 4,
        out_shape=[
            jax.ShapeDtypeStruct((32, 512), F32),
            sent_out(32, 512),
            sent_out(40, 512),
            sent_out(40, 512),
        ],
        scratch_shapes=[pltpu.VMEM((8, 40, 128), F32)],
        compiler_params=params(),
        cost_estimate=cost(1),
        name="split",
    )(sent)


def rows_kernel(own_ref, theirs_ref, out_ref):
    half = lax.axis_index("core")
    for ref, start in ((own_ref, 32 * half), (theirs_ref, 32 - 32 * half)):
        out_ref[pl.ds(pl.multiple_of(start, 32), 32)] = ref[...]


def join_rows(own, theirs):
    return pl.pallas_call(
        rows_kernel,
        in_specs=[VMEM, VMEM],
        out_specs=VMEM,
        out_shape=jax.ShapeDtypeStruct((64, 512), F32),
        compiler_params=params(),
        cost_estimate=cost(1),
        name="join_rows",
    )(own, theirs)


def join_kernel(own_ref, theirs_ref, out_ref):
    half = lax.axis_index("core")
    out_ref[...] = jnp.zeros((72, 512), F32)
    for ref, start in ((own_ref, 32 * half), (theirs_ref, 32 - 32 * half)):
        rows = pl.ds(pl.multiple_of(start, 32), 40)
        out_ref[rows] += ref[...]


def join(own, theirs):
    return pl.pallas_call(
        join_kernel,
        in_specs=[VMEM, VMEM],
        out_specs=VMEM,
        out_shape=jax.ShapeDtypeStruct((72, 512), F32),
        compiler_params=params(),
        cost_estimate=cost(1),
        name="join",
    )(in_hbm(own), theirs)


def spread_rows(scal_ref, q, step, ch, field, padded_ref, total_ref):
    padded_ref[ch, 8:40] = field
    low, mid, high = HALO + step, HALO, HALO - step
    value = (
        scal_ref[q, 0] * padded_ref[ch, low : low + 40]
        + scal_ref[q, 1] * padded_ref[ch, mid : mid + 40]
        + scal_ref[q, 2] * padded_ref[ch, high : high + 40]
    )
    for e in range(3):
        total_ref[SHIFTS.index((e - 1) * step), ch] += scal_ref[q, 3 + e] * value


def clear(padded_ref, total_ref):
    for ch in range(8):
        padded_ref[ch, 0:8] = jnp.zeros((8, 128), F32)
        padded_ref[ch, 40:48] = jnp.zeros((8, 128), F32)
        for d in range(7):
            total_ref[d, ch] = jnp.zeros((40, 128), F32)


def shift_all(total_ref, ch):
    lane = lanes_of((40, 128))
    main = total_ref[0, ch]
    edge = jnp.zeros((40, 128), F32)
    for d, col in enumerate(SHIFTS):
        if col:
            turned = pltpu.roll(total_ref[d, ch], col % 128, 1)
            inside = (lane >= col) if col > 0 else (lane < 128 + col)
            main = main + jnp.where(inside, turned, 0.0)
            edge = edge + jnp.where(inside, 0.0, turned)
    return main, edge


def shifted_columns(field_ref, turned_ref):
    lane = lanes_of((40, 128))

    @pl.loop(0, 8)
    def channel(ch):
        main = field_ref[ch, :40]
        edge = field_ref[ch, 40:]
        for d, col in enumerate(SHIFTS):
            if col:
                inside = (lane < 128 - col) if col > 0 else (lane >= -col)
                turned_ref[d, ch] = jnp.where(
                    inside, pltpu.roll(main, -col % 128, 1), pltpu.roll(edge, -col % 128, 1)
                )
            else:
                turned_ref[d, ch] = main


def each_level(scal_ref, q, work):
    for level, step in enumerate(STEPS):
        pl.when(scal_ref[q, 7] == F32(level + 1))(functools.partial(work, step))


def shrink(scal_ref, q, at, dual_ref, turned_ref, out_ref, after=None):
    def at_level(step):
        low, mid, high = (SHIFTS.index(s) for s in (-step, 0, step))
        squares = jnp.zeros((32, 128), F32)
        for ch in range(8):
            across = (
                scal_ref[q, 3] * turned_ref[low, ch]
                + scal_ref[q, 4] * turned_ref[mid, ch]
                + scal_ref[q, 5] * turned_ref[high, ch]
            )
            value = (
                scal_ref[q, 0] * across[HALO - step : HALO - step + 32]
                + scal_ref[q, 1] * across[HALO : HALO + 32]
                + scal_ref[q, 2] * across[HALO + step : HALO + step + 32]
            )
            raised = dual_ref[at, ch] + 0.5 * value
            out_ref[at, ch] = raised
            squares = squares + raised * raised
        limit = scal_ref[q, 6]
        scale = limit / jnp.maximum(jnp.sqrt(squares), limit)
        for ch in range(8):
            value = out_ref[at, ch] * scale
            out_ref[at, ch] = value
            if after is not None:
                after(step, ch, value)

    each_level(scal_ref, q, at_level)


class Scalars:
    def __init__(self, filters_ref, level_ref):
        self.filters_ref = filters_ref
        self.level_ref = level_ref

    def __getitem__(self, at):
        q, column = at
        if column == 7:
            return self.level_ref[q].astype(F32)
        return self.filters_ref[column % 3, column // 3, q]


def start_kernel(filters_ref, level_ref, image_ref, dual_ref, out_ref, padded_ref, total_ref):
    step_index = pl.program_id(0)
    scal_ref = Scalars(filters_ref, level_ref)

    @pl.when(step_index == 0)
    def first():
        clear(padded_ref, total_ref)

    @pl.loop(0, 3)
    def basis(i):
        q = 3 * step_index + i

        def at_level(step):
            for ch in range(8):
                spread_rows(scal_ref, q, step, ch, dual_ref[i, ch], padded_ref, total_ref)

        each_level(scal_ref, q, at_level)

    @pl.when(step_index == 2)
    def final():
        for ch in range(8):
            main, edge = shift_all(total_ref, ch)
            out_ref[ch, 0:32] = image_ref[ch]
            out_ref[ch, 32:72] = main
            out_ref[ch, 72:80] = packed_edge(edge)


TURNED = pltpu.VMEM((7, 8, 40, 128), F32)
FIELD = pltpu.VMEM((8, 80, 128), F32)
PADDED = pltpu.VMEM((8, 48, 128), F32)
THIRD = pl.BlockSpec((3, 8, 32, 128), lambda i: (i, 0, 0, 0))


def whole(*shape):
    return pl.BlockSpec(shape, lambda i: (0,) * len(shape))


def start(filters, levels, image, dual):
    return pl.pallas_call(
        start_kernel,
        grid=(3,),
        in_specs=[SMEM, SMEM, whole(8, 32, 128), THIRD],
        out_specs=whole(8, 80, 128),
        out_shape=sent_out(8, 80, 128),
        scratch_shapes=[PADDED, TURNED],
        compiler_params=params(),
        cost_estimate=cost(4),
        name="start",
    )(filters, in_hbm(levels), in_hbm(image), in_hbm(dual))


def middle_kernel(scal_ref, before_ref, pair_ref, dual_ref, dual_out, part_out, right_out, left_out,
                  now_out, field_ref, turned_ref, padded_ref, total_ref):
    step_index = pl.program_id(0)

    @pl.when(step_index == 0)
    def first():
        for ch in range(8):
            main = pair_ref[ch, :40]
            now_out[ch, :40] = main
            now = 2.0 * main
            field_ref[ch, 4:36] = now[4:36] - before_ref[ch]
            outer = pair_ref[ch, 56:64]
            field_ref[ch, 0:4] = now[0:4] - outer[0:4]
            field_ref[ch, 36:40] = now[36:40] - outer[4:8]
            edge = unpacked_edge(pair_ref[ch, 40:48])
            now_out[ch, 40:] = edge
            field_ref[ch, 40:] = 2.0 * edge - unpacked_edge(pair_ref[ch, 48:56])
        shifted_columns(field_ref, turned_ref)
        clear(padded_ref, total_ref)

    @pl.loop(0, 3)
    def basis(i):
        q = 3 * step_index + i

        def after(step, ch, value):
            spread_rows(scal_ref, q, step, ch, value, padded_ref, total_ref)

        shrink(scal_ref, q, i, dual_ref, turned_ref, dual_out, after)

    @pl.when(step_index == 2)
    def final():
        lane = lanes_of((40, 128))
        for ch in range(8):
            main, edge = shift_all(total_ref, ch)
            part_out[ch, :40] = main
            part_out[ch, 40:] = edge
            right_out[ch] = jnp.where(lane >= 128 - HALO, main, edge)
            left_out[ch] = jnp.where(lane < HALO, main, edge)


def middle(scal, dual, before, pair):
    side = jax.ShapeDtypeStruct((8, 40, 128), F32)
    field = sent_out(8, 80, 128)
    return pl.pallas_call(
        middle_kernel,
        grid=(3,),
        in_specs=[SMEM, whole(8, 32, 128), whole(8, 64, 128), THIRD],
        out_specs=[THIRD, whole(8, 80, 128)] + [whole(8, 40, 128)] * 2 + [whole(8, 80, 128)],
        out_shape=[sent_out(NBASIS, 8, 32, 128), field, side, side, field],
        scratch_shapes=[FIELD, TURNED, PADDED, TURNED],
        compiler_params=params(20),
        cost_estimate=cost(7),
        name="middle",
    )(scal, in_hbm(before), pair, in_hbm(dual))


def last_kernel(scal_ref, now_ref, part_ref, above_ref, below_ref, gradient_ref, dual_ref,
                image_out, dual_out, field_ref, turned_ref):
    step_index = pl.program_id(0)

    @pl.when(step_index == 0)
    def first():
        chip_row, facet = where_am_i()[2:]
        lane = lanes_of((40, 128))
        row = lax.broadcasted_iota(jnp.int32, (40, 128), 0) + (32 * chip_row - HALO)
        in_rows = (row >= 0) & (row < 512)
        in_edge = ((lane < HALO) & (facet < 7)) | ((lane >= 128 - HALO) & (facet > 0))
        for ch in range(8):
            for start, keep in ((0, in_rows), (40, in_rows & in_edge)):
                which = start // 40
                gradient = unpacked_edge(gradient_ref[ch, 40:]) if which else gradient_ref[ch, :40]
                field_ref[ch, start : start + 40] = part_ref[ch, start : start + 40] + gradient
                field_ref[ch, start : start + 8] += above_ref[ch, which]
                field_ref[ch, start + 32 : start + 40] += below_ref[ch, which]
                now = now_ref[ch, start : start + 40]
                value = jnp.maximum(now - 0.5 * field_ref[ch, start : start + 40], 0.0)
                value = jnp.where(keep, value, 0.0)
                if start == 0:
                    image_out[ch] = value[HALO : HALO + 32]
                field_ref[ch, start : start + 40] = 2.0 * value - now
        shifted_columns(field_ref, turned_ref)

    @pl.loop(0, 3)
    def basis(i):
        shrink(scal_ref, 3 * step_index + i, i, dual_ref, turned_ref, dual_out)


def last(scal, dual, now, part, above, below, gradient):
    field, side = whole(8, 80, 128), whole(8, 2, 8, 128)
    return pl.pallas_call(
        last_kernel,
        grid=(3,),
        in_specs=[SMEM, field, field, side, side, whole(8, 48, 128), THIRD],
        out_specs=[whole(8, 32, 128), THIRD],
        out_shape=[
            jax.ShapeDtypeStruct((8, 32, 128), F32),
            jax.ShapeDtypeStruct((NBASIS, 8, 32, 128), F32),
        ],
        scratch_shapes=[FIELD, TURNED],
        compiler_params=params(20),
        cost_estimate=cost(4),
        name="last",
    )(scal, now, part, above, below, gradient, dual)


def swapped(value):
    return lax.ppermute(value, "core", [(0, 1), (1, 0)])


def gathered(value):
    return gathered_x(value) + gathered_x(across_y(value))


def to_chips(pieces):
    arrived = [pieces[0]]
    for i in range(1, 8):
        route = [
            (4 * y + x, 4 * (y ^ (i // 4)) + (x + i) % 4) for y in range(2) for x in range(4)
        ]
        arrived.append(lax.ppermute(pieces[i], CHIPS, route))
    return arrived


def across_y(value):
    return lax.ppermute(value, "y", [(0, 1), (1, 0)])


def along_x(value, step):
    return lax.ppermute(value, "x", [(i, (i + step) % 4) for i in range(4)])


def gathered_x(value):
    return [value] + [along_x(value, -ahead) for ahead in (1, 2, 3)]


def neighbours(value, axis, count, step):
    return lax.ppermute(
        value, axis, [(i, i + step) for i in range(count) if 0 <= i + step < count]
    )


def half_of(value, half, size, dim):
    return lax.dynamic_slice_in_dim(value, half * size, size, dim)


def per_device(
    sky_image,
    dual_coefs,
    phase_screen,
    grid_rows,
    grid_weight,
    visibilities,
    filters,
    level_counts,
    radius,
):
    half = lax.axis_index("core")
    scal = jnp.concatenate(
        [filters.reshape(NBASIS, 6), radius[:, None], level_counts[:, None].astype(F32)], axis=1
    )

    packed = start(filters.transpose(2, 1, 0), level_counts, sky_image, dual_coefs)

    weight_own = grid_weight[0, 0]
    weight_other, phase, packed = lax.optimization_barrier(
        (swapped(weight_own), phase_screen[0, 0], packed)
    )
    sent = lax.all_to_all(packed, "chan", 0, 0, tiled=True)
    phase_other = half_of(phase, 1 - half, 512, 1)
    data_own = visibilities[0, 0].reshape(128, 256)
    data = jnp.stack([data_own, swapped(data_own)])
    rows_own = grid_rows[0, 0]
    rows_other = swapped(rows_own.astype(F32)).astype(jnp.int32)
    left, right = tables(jnp.stack([rows_own, rows_other]))
    grid = gridding(weight_own, weight_other)
    sent, grid, phase_other = lax.optimization_barrier((sent, grid, swapped(phase_other)))
    trig = screens(phase, phase_other)

    own, other, term_own, term_other = split(sent)
    strip = join_rows(own, swapped(other))
    pieces = gathered(strip)
    extra = join(term_own, swapped(term_other))
    pieces, extra, data = lax.optimization_barrier((pieces, extra, data))

    seen, seen_copy, window = forward(pieces, trig, left, grid, True)
    sent = backward(seen_copy, swapped(seen), data, grid, right, trig, extra)
    sent = to_chips(sent)
    own, other, core = update(sent, window)

    pieces = gathered(core)
    packed = pair_to_facets(own, swapped(other))
    packed, pieces[4] = lax.optimization_barrier((packed, pieces[4]))
    pair = lax.all_to_all(packed, "chan", 0, 0, tiled=True)
    seen, seen_copy = forward(pieces, trig, left, grid, False)
    dual, part, to_right, to_left, now = middle(scal, dual_coefs, sky_image, pair)
    sent = backward(seen_copy, swapped(seen), data, grid, right, trig)
    windows = total_windows(lax.all_to_all(sent, CHIPS, 0, 0, tiled=True))
    from_left = neighbours(to_right, "chan", 8, 1)
    from_right = neighbours(to_left, "chan", 8, -1)
    packed = to_facets(*windows)
    from_left, from_right = lax.optimization_barrier((from_left, from_right, packed))[:2]
    lane = lanes_of((8, 40, 128))
    main = part[:, :40] + jnp.where(lane < HALO, from_left, 0.0)
    main = main + jnp.where(lane >= 128 - HALO, from_right, 0.0)
    edge = part[:, 40:] + jnp.where(lane >= 128 - HALO, from_left, 0.0)
    edge = edge + jnp.where(lane < HALO, from_right, 0.0)
    both = jnp.stack([main, edge], axis=1)
    above = neighbours(both[:, :, 32:], ("y", "x", "core"), 16, 1)
    below = neighbours(both[:, :, :8], ("y", "x", "core"), 16, -1)
    gradient = lax.all_to_all(packed, "chan", 0, 0, tiled=True)
    return tuple(last(scal, dual, now, both.reshape(8, 80, 128), above, below, gradient))


def solution(mesh):
    fine = Mesh(mesh.devices.reshape(8, 2, 4, 2), ("chan", "y", "x", "core"))
    rows = ("y", "x", "core")
    placed = (
        P(None, rows, "chan"),
        P(None, None, rows, "chan"),
        P("chan", rows, None, None),
        P("chan", rows, None),
        P("chan", rows, None, None),
        P("chan", rows, None, None, None),
        P(),
        P(),
        P(),
    )
    return jax.shard_map(
        per_device,
        mesh=fine,
        in_specs=placed,
        out_specs=(P(None, rows, "chan"), P(None, None, rows, "chan")),
        check_vma=False,
    )
```
